256 devices in a mesh: seq: 32 (over x, z_lo, y), dp: 8 (over z_hi, core).
Axes of the slice: x: 4, y: 4, z: 8 (z_hi: 4, z_lo: 2; z = z_hi * 2 + z_lo), core: 2. Of those that a mesh axis runs over, the one named last changes fastest.
Arguments:
- normed_input: bfloat16 [8, 4096, 5120], P('dp', 'seq'), may hold values from -6 to 6
- query_states: bfloat16 [8, 4096, 4096], P('dp', 'seq'), may hold values from -6 to 6
- rotated_key_states: bfloat16 [8, 4096, 512], P('dp', 'seq'), may hold values from -6 to 6
- value_state_rows: bfloat16 [8, 4096, 512], P('dp', 'seq'), may hold values from -6 to 6
- attn_output: bfloat16 [8, 4096, 4096], P('dp', 'seq'), may hold values from -6 to 6
- output_grad: bfloat16 [8, 4096, 4096], P('dp', 'seq'), may hold values from -6 to 6
Outputs:
- query_grad: bfloat16 [8, 4096, 4096], P('dp', 'seq')
- key_gradient: bfloat16 [8, 4096, 512], P('dp', 'seq')
- value_gradient: bfloat16 [8, 4096, 512], P('dp', 'seq')
- weight_grad: float32 [5120, 512], P(('seq', 'dp'))
The draws below stay inside these ranges and needn't reach their ends.
All inputs are finite; a program needn't handle non-finite values.
Results may differ from the reference program's by a relative error of at most 0.012.
Values may be sent and summed in bfloat16 or wider, within the bound.
A program may use at most 128 MiB of HBM per device.

```python
import jax
import jax.numpy as jnp
from jax import lax

MODEL_WIDTH = 5120
QUERY_HEADS = 32
KEY_VALUE_HEADS = 4
HEAD_SIZE = 128
REPLICA_COUNT = 8
SEQUENCE_LENGTH = 4096


def draw_query_states(key, part):
    key = jax.random.fold_in(key, 5)
    drawn_values = jnp.clip(jax.random.normal(key, (REPLICA_COUNT, SEQUENCE_LENGTH, QUERY_HEADS * HEAD_SIZE), jnp.float32), -6.0, 6.0)
    return drawn_values.astype(jnp.bfloat16)


def draw_rotated_key_states(key, part):
    key = jax.random.fold_in(key, 9)
    drawn_values = jnp.clip(jax.random.normal(key, (REPLICA_COUNT, SEQUENCE_LENGTH, KEY_VALUE_HEADS * HEAD_SIZE), jnp.float32), -6.0, 6.0)
    return drawn_values.astype(jnp.bfloat16)


def with_spikes(drawn, own_key, source, target, shards_of, factor):
    owner, partner = [(jnp.arange(drawn.shape[axis_at]) // (drawn.shape[axis_at] // shards_of)).reshape([-1 if axis == axis_at else 1 for axis in range(drawn.ndim)]) for axis_at in (source, target)]
    chosen = jax.random.permutation(own_key, shards_of)[partner]
    strong = (owner == chosen) | (owner == (partner + shards_of // 2) % shards_of)
    return jnp.where(strong, factor * drawn, drawn)


def levels(key, dims, cuts, least, largest):
    loudness, own = 1.0, jax.random.fold_in(key, 6)
    for dim, shards_of in cuts:
        steps = jnp.exp(jax.random.uniform(jax.random.fold_in(own, dim), (shards_of,), jnp.float32, least / len(cuts), largest / len(cuts)))
        loudness = loudness * jnp.repeat(steps, dims[dim] // shards_of).reshape([-1 if axis == dim else 1 for axis in range(len(dims))])
    return loudness


def noise(stream_key, shape, spread, most, cuts=(), kind=jnp.bfloat16):
    factor_of = levels(stream_key, shape, cuts, -0.22, 0.18) if cuts else 1.0
    drawn = jax.random.normal(stream_key, shape, jnp.float32) * spread * factor_of
    return jnp.minimum(jnp.maximum(drawn, -most), most).astype(kind)


def gaussian_with(stream_key, shape, deviation, most, cuts, heavy, kind=jnp.bfloat16):
    array = deviation * jax.random.normal(stream_key, shape, jnp.float32)
    if cuts:
        array = array * levels(stream_key, shape, cuts, -0.22, 0.18)
    return jnp.clip(with_spikes(array, jax.random.fold_in(stream_key, 3), *heavy), -most, most).astype(kind)


def setup_inputs(seed: int = 0) -> dict:
    seeds = jax.random.split(jax.random.key(seed), 7)
    normed_input = gaussian_with(seeds[0], (REPLICA_COUNT, SEQUENCE_LENGTH, MODEL_WIDTH), 1.0, 6.0, ((0, 8), (1, 32)), (1, 2, 32, 2.75))
    query_states = draw_query_states(jax.random.fold_in(seeds[6], 71), 0)
    rotated_key_states = draw_rotated_key_states(jax.random.fold_in(seeds[6], 71), 0)
    value_state_rows = noise(seeds[3], (REPLICA_COUNT, SEQUENCE_LENGTH, KEY_VALUE_HEADS * HEAD_SIZE), 1.0, 6.0, ((0, 8), (1, 32)))
    attn_output = noise(seeds[4], (REPLICA_COUNT, SEQUENCE_LENGTH, QUERY_HEADS * HEAD_SIZE), 1.0, 6.0, ((0, 8), (1, 32)))
    output_grad = noise(seeds[5], (REPLICA_COUNT, SEQUENCE_LENGTH, QUERY_HEADS * HEAD_SIZE), 1.0, 6.0, ((0, 8), (1, 32)))
    return dict(normed_input=normed_input, query_states=query_states, rotated_key_states=rotated_key_states, value_state_rows=value_state_rows, attn_output=attn_output, output_grad=output_grad)


def head_backward(query_rows, key_rows, value_rows, output_rows, grad_rows):
    score_scale = HEAD_SIZE ** -0.5
    length = query_rows.shape[0]
    scores = jnp.dot(query_rows, key_rows.T, preferred_element_type=jnp.float32) * score_scale
    places = jnp.arange(length, dtype=jnp.int32)
    visible = places[None, :] <= places[:, None]
    scores = jnp.where(visible, scores, -jnp.inf)
    row_max = jnp.max(scores, axis=1, keepdims=True)
    exp_scores = jnp.exp(scores - row_max)
    weights = exp_scores / jnp.sum(exp_scores, axis=1, keepdims=True)
    weights_low = weights.astype(jnp.bfloat16)
    value_portion = jnp.dot(weights_low.T, grad_rows, preferred_element_type=jnp.float32)
    prob_grads = jnp.dot(grad_rows, value_rows.T, preferred_element_type=jnp.float32)
    row_delta = jnp.sum(grad_rows.astype(jnp.float32) * output_rows.astype(jnp.float32), axis=1, keepdims=True)
    score_grads = (weights * (prob_grads - row_delta) * score_scale).astype(jnp.bfloat16)
    query_part = jnp.dot(score_grads, key_rows, preferred_element_type=jnp.float32).astype(jnp.bfloat16)
    key_portion = jnp.dot(score_grads.T, query_rows, preferred_element_type=jnp.float32)
    return query_part, key_portion, value_portion


def reference(normed_input, query_states, rotated_key_states, value_state_rows, attn_output, output_grad):
    group_width = QUERY_HEADS // KEY_VALUE_HEADS
    query_list = []
    key_pieces = []
    value_list = []
    weight_gradient_total = jnp.zeros((MODEL_WIDTH, KEY_VALUE_HEADS * HEAD_SIZE), jnp.float32)
    for replica in range(REPLICA_COUNT):
        def divided_heads(source, head_count):
            return source[replica].reshape(SEQUENCE_LENGTH, head_count, HEAD_SIZE).transpose(1, 0, 2)

        query_heads = divided_heads(query_states, QUERY_HEADS)
        key_head_rows = jnp.repeat(divided_heads(rotated_key_states, KEY_VALUE_HEADS), group_width, axis=0)
        value_head_rows = jnp.repeat(divided_heads(value_state_rows, KEY_VALUE_HEADS), group_width, axis=0)
        output_heads = divided_heads(attn_output, QUERY_HEADS)
        grad_heads = divided_heads(output_grad, QUERY_HEADS)
        query_part, key_portion, value_portion = lax.map(
            lambda head_items: head_backward(*head_items),
            (query_heads, key_head_rows, value_head_rows, output_heads, grad_heads))
        key_gradient_sum = key_portion.reshape(KEY_VALUE_HEADS, group_width, SEQUENCE_LENGTH, HEAD_SIZE).sum(axis=1).astype(jnp.bfloat16)
        value_gradient_sum = value_portion.reshape(KEY_VALUE_HEADS, group_width, SEQUENCE_LENGTH, HEAD_SIZE).sum(axis=1).astype(jnp.bfloat16)
        query_list.append(query_part.transpose(1, 0, 2).reshape(SEQUENCE_LENGTH, QUERY_HEADS * HEAD_SIZE))
        key_pieces.append(key_gradient_sum.transpose(1, 0, 2).reshape(SEQUENCE_LENGTH, KEY_VALUE_HEADS * HEAD_SIZE))
        flattened_value = value_gradient_sum.transpose(1, 0, 2).reshape(SEQUENCE_LENGTH, KEY_VALUE_HEADS * HEAD_SIZE)
        value_list.append(flattened_value)
        weight_gradient_total = weight_gradient_total + jnp.dot(normed_input[replica].T, flattened_value, preferred_element_type=jnp.float32)
    return jnp.stack(query_list), jnp.stack(key_pieces), jnp.stack(value_list), weight_gradient_total
```

```python
import functools
import jax, jax.numpy as jnp
from jax import lax
from jax.sharding import Mesh, PartitionSpec as P
from jax.experimental import pallas as pl
from jax.experimental.pallas import tpu as pltpu
bf=jnp.bfloat16; f32=jnp.float32
HEADS=8; D=128; ROWS=128; LANES=HEADS*ROWS
SCALE=D**-0.5
LOG=SCALE*1.4426950408889634
def dot(a,b,ca,cb):
    return lax.dot_general(a,b,(((ca,),(cb,)),((),())),preferred_element_type=f32)

def attn_kernel(C, pos, qg, k, v, dq, dk, dv, qt, gt, qn, gn, kt, S, E, dka, dva, dqt):
    T=k.shape[0]
    for t in range(T//128):
        kt[:,t*128:(t+1)*128]=k[t*128:(t+1)*128,:].T
    dka[...]=jnp.zeros_like(dka)
    dva[...]=jnp.zeros_like(dva)
    def block(b,carry):
        i=pos[b]
        for h in range(HEADS):
            cs=slice(h*128,(h+1)*128)
            qh=qg[b,:,cs]
            qt[:,cs]=qh.T
            qn[cs,:]=qh
        d3=qg[b,:,2048+256:2048+384].astype(f32).T
        d8=d3[0:8]+d3[8:16]+d3[16:24]
        delta=jnp.concatenate([d8[h:h+1] for h in range(HEADS)],axis=1)
        n=i//(C//128)
        def score(ch,w):
            at=pl.ds(pl.multiple_of(ch*w,w),w)
            return dot(k[at,:],qt[...],1,0)
        def p1(ch,m):
            s=score(ch,C)
            S[pl.ds(pl.multiple_of(ch*C,C),C),:]=s
            return jnp.maximum(m,jnp.max(s.reshape(C//8,8,LANES),axis=0))
        m=lax.fori_loop(0,n,p1,jnp.full((8,LANES),-1e30,f32))
        s=score(n,C)
        key=n*C+lax.broadcasted_iota(jnp.int32,(C,LANES),0)
        qp=i*128+lax.rem(lax.broadcasted_iota(jnp.int32,(C,LANES),1),128)
        s=jnp.where(key<=qp,s,-1e30)
        S[pl.ds(pl.multiple_of(n*C,C),C),:]=s
        m=jnp.maximum(m,jnp.max(s.reshape(C//8,8,LANES),axis=0))
        mc=jnp.max(m,axis=0,keepdims=True)*LOG
        def p2(ch,l):
            at=pl.ds(pl.multiple_of(ch*C,C),C)
            e=jnp.exp2(S[at,:]*LOG-mc)
            E[at,:]=e.astype(bf)
            return l+jnp.sum(e.reshape(C//8,8,LANES),axis=0)
        l=lax.fori_loop(0,n+1,p2,jnp.zeros((8,LANES),f32))
        r=1.0/jnp.sum(l,axis=0,keepdims=True)
        dr=delta*r
        for h in range(HEADS):
            cs=slice(h*128,(h+1)*128)
            gh=(qg[b,:,1024+h*128:1024+(h+1)*128].astype(f32).T*r[:,cs]).astype(bf)
            gt[:,cs]=gh
            gn[cs,:]=gh.T
        dqt[...]=jnp.zeros_like(dqt)
        def p3(ch,c):
            at=pl.ds(pl.multiple_of(ch*C,C),C)
            e=E[at,:]
            dp=dot(v[at,:],gt[...],1,0)
            ds=(e.astype(f32)*(dp-dr)).astype(bf)
            dva[at,:]+=dot(e,gn[...],1,0)
            dka[at,:]+=dot(ds,qn[...],1,0)
            dqt[...]+=dot(kt[:,at],ds,1,0)
            return c
        lax.fori_loop(0,n+1,p3,0)
        for h in range(HEADS):
            cs=slice(h*128,(h+1)*128)
            dq[b,:,cs]=(dqt[:,cs].T*SCALE).astype(bf)
        return carry
    lax.fori_loop(0,4,block,0)
    dk[...]=(dka[...]*SCALE).astype(bf)
    dv[...]=dva[...].astype(bf)

def attn(pos,qg,k,v,C=512):
    T=k.shape[0]
    vm=pl.BlockSpec(memory_space=pltpu.VMEM)
    return pl.pallas_call(functools.partial(attn_kernel, C),
        out_shape=(jax.ShapeDtypeStruct((4,128,1024),bf),jax.ShapeDtypeStruct((T,128),bf),jax.ShapeDtypeStruct((T,128),bf)),
        in_specs=[pl.BlockSpec(memory_space=pltpu.SMEM),vm,vm,vm],out_specs=(vm,vm,vm),
        scratch_shapes=[pltpu.VMEM((128,LANES),bf),pltpu.VMEM((128,LANES),bf),pltpu.VMEM((LANES,128),bf),pltpu.VMEM((LANES,128),bf),
          pltpu.VMEM((128,T),bf),pltpu.VMEM((T,LANES),f32),pltpu.VMEM((T,LANES),bf),pltpu.VMEM((T,128),f32),pltpu.VMEM((T,128),f32),pltpu.VMEM((128,LANES),f32)],
        compiler_params=pltpu.CompilerParams(vmem_limit_bytes=60<<20),name="attention_backward")(pos,qg,k,v)


def per_device(x_in, q, k, v, o, g):
    j = lax.axis_index("x")
    z = lax.axis_index("z")
    y = lax.axis_index("y")
    q, g, o, k, v, x_in = (a[0] for a in (q, g, o, k, v, x_in))
    delta = jnp.sum((g.astype(f32) * o.astype(f32)).reshape(ROWS, 4, HEADS, D), axis=3)
    d0 = delta.astype(bf)
    r1 = delta - d0.astype(f32)
    d1 = r1.astype(bf)
    d2 = (r1 - d1.astype(f32)).astype(bf)
    parts = [q.reshape(ROWS, 4, LANES), g.reshape(ROWS, 4, LANES), k.reshape(ROWS, 4, D), v.reshape(ROWS, 4, D),
             d0, d1, d2, jnp.zeros((ROWS, 4, 104), bf)]
    send = jnp.concatenate(parts, axis=2).transpose(1, 0, 2)
    x_send = x_in.reshape(ROWS, 4, -1).transpose(1, 0, 2)

    def perm(d):
        return [(x * 2 + zz, ((x + d) % 4) * 2 + (zz ^ (x & 1))) for x in range(4) for zz in range(2)]

    def back(d):
        return [(b, a) for a, b in perm(d)]

    def pick(a, i):
        return lax.dynamic_index_in_dim(a, i, 0, keepdims=False)

    got = jnp.stack([lax.ppermute(pick(send, (j + d) % 4), ("x", "z"), perm(d)) for d in range(4)])
    x_got = [lax.ppermute(pick(x_send, (j + d) % 4), ("x", "z"), perm(d)) for d in range(4)]
    pos = jnp.stack([8 * s + 4 * (z ^ (s & 1)) + y for s in [(j - d) % 4 for d in range(4)]]).astype(jnp.int32)

    def by_source(a):
        return jnp.stack([pick(a, (j - s) % 4) for s in range(4)])

    kv = by_source(got[:, :, 2 * LANES:2 * LANES + 2 * D])
    kv = lax.all_gather(kv, ("z", "y"), axis=0, tiled=False).reshape(2, 4, 4, ROWS, 2 * D)
    kv = jnp.stack([kv[::-1, :, s] if s % 2 else kv[:, :, s] for s in range(4)]).reshape(-1, 2 * D)
    dq, dk, dv = attn(pos, got, kv[:, :D], kv[:, D:])
    dqb = [lax.ppermute(dq[d], ("x", "z"), back(d)) for d in range(4)]
    dkv = jnp.concatenate([dk, dv], axis=1).reshape(4, 2, 4, ROWS, 2 * D)
    dkv = jnp.stack([dkv[s, ::-1] if s % 2 else dkv[s] for s in range(4)], axis=2).reshape(8, 4, ROWS, 2 * D)
    dkv = lax.all_to_all(dkv, ("z", "y"), 0, 0, tiled=True).astype(f32).sum(axis=0).astype(bf)
    dkvb = [lax.ppermute(pick(dkv, (j - d) % 4), ("x", "z"), back(d)) for d in range(4)]

    def by_group(parts):
        a = jnp.stack(parts)
        return jnp.stack([pick(a, (s - j) % 4) for s in range(4)], axis=1)

    dq_out = by_group(dqb).reshape(1, ROWS, -1)
    dkv_out = by_group(dkvb)
    dk_out = dkv_out[:, :, :D].reshape(1, ROWS, -1)
    dv_out = dkv_out[:, :, D:].reshape(1, ROWS, -1)
    dv_all = lax.all_gather(dkv[:, :, D:], "x", axis=0, tiled=False)
    dv_all = dv_all.transpose(1, 2, 0, 3).reshape(4 * ROWS, 4 * D)
    x_all = by_source(jnp.stack(x_got)).reshape(4 * ROWS, -1)
    w = dot(x_all, dv_all, 0, 0).astype(bf)
    w = lax.all_to_all(w.reshape(64, -1, 4 * D), ("z", "y", "h", "c"), 0, 0, tiled=True)
    return dq_out, dk_out, dv_out, w.astype(f32).sum(axis=0)


def solution(mesh):
    fine = Mesh(mesh.devices.reshape(4, 2, 4, 4, 2), ("x", "z", "y", "h", "c"))
    seq, dp = ("x", "z", "y"), ("h", "c")
    rows = P(dp, seq, None)
    return jax.shard_map(per_device, mesh=fine, in_specs=(rows,) * 6,
                         out_specs=(rows, rows, rows, P(seq + dp, None)), check_vma=False)
```

```python
import jax
import jax.numpy as jnp
from jax import lax
from jax.sharding import Mesh, PartitionSpec as P
from jax.experimental import pallas as pl
from jax.experimental.pallas import tpu as pltpu

bf = jnp.bfloat16
f32 = jnp.float32
HEADS = 8
D = 128
ROWS = 128
LANES = HEADS * ROWS
SCALE = D ** -0.5
LOG = SCALE * 1.4426950408889634
CHUNK = 512
BLOCKS = CHUNK // ROWS
XCOLS = 1280


def dot(a, b, ca, cb):
    return lax.dot_general(a, b, (((ca,), (cb,)), ((), ())), preferred_element_type=f32)


def cols(index, width):
    return pl.ds(pl.multiple_of(index * width, width), width)


def remote(src, dst, sems, at, peer):
    return pltpu.make_async_remote_copy(src_ref=src, dst_ref=dst, send_sem=sems[0].at[at], recv_sem=sems[1].at[at],
                                        device_id=peer, device_id_type=pl.DeviceIdType.MESH)


def arrived(ref, sem):
    pltpu.make_async_copy(ref, ref, sem).wait()


def kernel(q, g, o, k, v, xin, dqo, dko, dvo, xr, dvall,
           kv, kt, qr, gr, dr, gl, ol, dl, qt, gt, qn, gn, S, E, dka, dva, dqt, dqv, part, rcv, fin,
           *sems):
    (lg, lo), sk, sv, sq, sg, sd, sx, sb, sc, sdq, sp, srk, srv, sdv = [sems[i:i + 2] for i in range(0, 28, 2)]
    x, z, y = (lax.axis_index(a) for a in ("x", "z", "y"))
    me = 8 * x + 4 * z + y
    xs = [lax.rem(x + d, 4) for d in range(4)]
    ys = [lax.rem(y + e, 4) for e in range(4)]
    plane = [(dz, e) for dz in range(2) for e in range(4) if dz or e]

    def in_plane(dz, e):
        return {"z": (1 - z) if dz else z, "y": ys[e]}

    barrier = pltpu.get_barrier_semaphore()
    for d in (1, 2, 3):
        pl.semaphore_signal(barrier, inc=1, device_id={"x": xs[d]}, device_id_type=pl.DeviceIdType.MESH)
    for dz, e in plane:
        pl.semaphore_signal(barrier, inc=1, device_id=in_plane(dz, e), device_id_type=pl.DeviceIdType.MESH)
    get_g = pltpu.make_async_copy(g.at[0], gl, lg)
    get_o = pltpu.make_async_copy(o.at[0], ol, lo)
    get_g.start()
    get_o.start()
    pl.semaphore_wait(barrier, 10)

    sends = []

    def send(*a):
        copy = remote(*a)
        copy.start()
        sends.append(copy)

    for src, dst, s, width in ((k.at[0], kv.at[me, :, 0:D], sk, D), (v.at[0], kv.at[me, :, D:2 * D], sv, D),
                               (q.at[0], qr.at[x], sq, LANES), (g.at[0], gr.at[x], sg, LANES)):
        for d in (1, 3, 2):
            send(src.at[:, cols(xs[d], width)], dst, s, d, {"x": xs[d]})
        pltpu.make_async_copy(src.at[:, cols(x, width)], dst, s[1].at[0]).start()

    get_g.wait()
    get_o.wait()
    head = lax.broadcasted_iota(jnp.int32, (HEADS, LANES), 0)
    ones = jnp.where(head == lax.broadcasted_iota(jnp.int32, (HEADS, LANES), 1) // D, 1.0, 0.0).astype(bf)
    for j in range(4):
        at = slice(j * LANES, (j + 1) * LANES)
        prod = gl[:, at].astype(f32) * ol[:, at].astype(f32)
        high = prod.astype(bf)
        low = (prod - high.astype(f32)).astype(bf)
        dl[j] = dot(ones, high, 1, 1) + dot(ones, low, 1, 1)
    for d in (1, 3, 2):
        send(dl.at[xs[d]], dr.at[x], sd, d, {"x": xs[d]})
    pltpu.make_async_copy(dl.at[x], dr.at[x], sd[1].at[0]).start()

    def slot(s, zz, yy):
        return kv.at[8 * s + 4 * zz + yy]

    for s in range(4):
        d = lax.rem(x + 4 - s, 4)
        mine = slot(s, z, y)
        arrived(mine.at[:, 0:D], sk[1].at[d])
        arrived(mine.at[:, D:2 * D], sv[1].at[d])
        send(mine, mine, sb, s, {"z": 1 - z})
        for e in (1, 3, 2):
            send(mine, mine, sc, (s, 0, e), {"y": ys[e]})
    for s in range(4):
        theirs = slot(s, 1 - z, y)
        arrived(theirs, sb[1].at[s])
        for e in (1, 3, 2):
            send(theirs, theirs, sc, (s, 1, e), {"y": ys[e]})
    for d in (1, 3, 2):
        send(xin.at[0, :, cols(xs[d], XCOLS)], xr.at[x], sx, d, {"x": xs[d]})
    pltpu.make_async_copy(xin.at[0, :, cols(x, XCOLS)], xr.at[x], sx[1].at[0]).start()

    dka[...] = jnp.zeros_like(dka)
    dva[...] = jnp.zeros_like(dva)

    def block(s, carry):
        d = lax.rem(x + 4 - s, 4)
        i = 8 * s + 4 * z + y
        for e in (1, 2, 3):
            yy = lax.rem(y + 4 - e, 4)
            arrived(slot(s, z, yy), sc[1].at[s, 0, e])
            arrived(slot(s, 1 - z, yy), sc[1].at[s, 1, e])
        for b in range(8):
            kt[:, cols(8 * s + b, D)] = kv[8 * s + b, :, 0:D].T
        arrived(qr.at[s], sq[1].at[d])
        arrived(gr.at[s], sg[1].at[d])
        arrived(dr.at[s], sd[1].at[d])
        for h in range(HEADS):
            cs = slice(h * D, (h + 1) * D)
            qh = qr[s, :, cs]
            qt[:, cs] = qh.T
            qn[cs, :] = qh
        delta = jnp.concatenate([dr[s, h:h + 1, :] for h in range(HEADS)], axis=1)
        n = i // BLOCKS

        def score(ch):
            keys = kv[pl.ds(ch * BLOCKS, BLOCKS), :, 0:D].reshape(CHUNK, D)
            return dot(keys, qt[...], 1, 0)

        def top(m, s):
            return jnp.maximum(m, jnp.max(s.reshape(CHUNK // 8, 8, LANES), axis=0))

        def p1(ch, m):
            s = score(ch)
            S[cols(ch, CHUNK), :] = s
            return top(m, s)

        m = lax.fori_loop(0, n, p1, jnp.full((8, LANES), -1e30, f32))
        last = score(n)
        key = n * CHUNK + lax.broadcasted_iota(jnp.int32, (CHUNK, LANES), 0)
        row = i * ROWS + lax.broadcasted_iota(jnp.int32, (CHUNK, LANES), 1) % ROWS
        last = jnp.where(key <= row, last, -1e30)
        S[cols(n, CHUNK), :] = last
        mc = jnp.max(top(m, last), axis=0, keepdims=True) * LOG

        def p2(ch, total):
            e = jnp.exp2(S[cols(ch, CHUNK), :] * LOG - mc)
            E[cols(ch, CHUNK), :] = e.astype(bf)
            return total + jnp.sum(e.reshape(CHUNK // 8, 8, LANES), axis=0)

        total = lax.fori_loop(0, n + 1, p2, jnp.zeros((8, LANES), f32))
        r = 1.0 / jnp.sum(total, axis=0, keepdims=True)
        shift = delta * r
        for h in range(HEADS):
            cs = slice(h * D, (h + 1) * D)
            gh = (gr[s, :, cs].astype(f32).T * r[:, cs]).astype(bf)
            gt[:, cs] = gh
            gn[cs, :] = gh.T
        dqt[...] = jnp.zeros_like(dqt)

        def p3(ch, c):
            at = cols(ch, CHUNK)
            e = E[at, :]
            values = kv[pl.ds(ch * BLOCKS, BLOCKS), :, D:2 * D].reshape(CHUNK, D)
            ds = (e.astype(f32) * (dot(values, gt[...], 1, 0) - shift)).astype(bf)
            dva[at, :] += dot(e, gn[...], 1, 0)
            dka[at, :] += dot(ds, qn[...], 1, 0)
            dqt[...] += dot(kt[:, at], ds, 1, 0)
            return c

        lax.fori_loop(0, n + 1, p3, 0)
        for h in range(HEADS):
            cs = slice(h * D, (h + 1) * D)
            dqv[s, :, cs] = (dqt[:, cs].T * SCALE).astype(bf)

        home = dqo.at[0, :, cols(x, LANES)]

        @pl.when(s == x)
        def _():
            pltpu.make_async_copy(dqv.at[s], home, sdq[1].at[0]).start()

        @pl.when(s != x)
        def _():
            remote(dqv.at[s], home, sdq, lax.rem(s + 4 - x, 4), {"x": s}).start()

        return carry

    lax.fori_loop(0, 4, block, 0)

    for b in range(32):
        at = slice(b * ROWS, (b + 1) * ROWS)
        part[b // 8, b % 8, :, 0:D] = (dka[at, :] * SCALE).astype(bf)
        part[b // 8, b % 8, :, D:2 * D] = dva[at, :].astype(bf)
    for dz, e in plane:
        peer = in_plane(dz, e)
        send(part.at[:, 4 * peer["z"] + peer["y"]], rcv.at[dz * 4 + e], sp, dz * 4 + e, peer)
    for s in range(4):
        fin[s] = part[s, 4 * z + y].astype(f32)
    for dz, e in plane:
        arrived(rcv.at[dz * 4 + e], sp[1].at[dz * 4 + e])
        for s in range(4):
            fin[s] += rcv[dz * 4 + e, s].astype(f32)
    for s in range(4):
        part[s, 4 * z + y] = fin[s].astype(bf)
    out = part.at[:, 4 * z + y]
    for d in (1, 3, 2):
        t = xs[d]
        send(out.at[:, :, D:2 * D], dvall.at[:, :, cols(x, D)], sdv, d, {"x": t})
        send(out.at[t, :, 0:D], dko.at[0, :, cols(x, D)], srk, d, {"x": t})
        send(out.at[t, :, D:2 * D], dvo.at[0, :, cols(x, D)], srv, d, {"x": t})
    own = [pltpu.make_async_copy(out.at[:, :, D:2 * D], dvall.at[:, :, cols(x, D)], sdv[1].at[0]),
           pltpu.make_async_copy(out.at[x, :, 0:D], dko.at[0, :, cols(x, D)], srk[1].at[0]),
           pltpu.make_async_copy(out.at[x, :, D:2 * D], dvo.at[0, :, cols(x, D)], srv[1].at[0])]
    for copy in own:
        copy.start()
    for d in range(4):
        f = lax.rem(x + 4 - d, 4)
        arrived(xr.at[f], sx[1].at[d])
        arrived(dqo.at[0, :, cols(f, LANES)], sdq[1].at[d])
        arrived(dvall.at[:, :, cols(f, D)], sdv[1].at[d])
        arrived(dko.at[0, :, cols(f, D)], srk[1].at[d])
        arrived(dvo.at[0, :, cols(f, D)], srv[1].at[d])
    for copy in sends:
        copy.wait_send()
    for d in (1, 2, 3):
        remote(dqv.at[xs[d]], dqo.at[0, :, cols(x, LANES)], sdq, d, {"x": xs[d]}).wait_send()


def whole(q, g, o, k, v, xin):
    T = 32 * ROWS
    anyspace = pl.BlockSpec(memory_space=pl.ANY)
    dma = pltpu.SemaphoreType.DMA
    shapes = [(), ()] + [(4,)] * 14 + [(4, 2, 4)] * 2 + [(4,)] * 2 + [(8,)] * 2 + [(4,)] * 6
    scratch = [((32, ROWS, 2 * D), bf), ((D, T), bf), ((4, ROWS, LANES), bf), ((4, ROWS, LANES), bf), ((4, HEADS, ROWS), f32),
               ((ROWS, 4 * LANES), bf), ((ROWS, 4 * LANES), bf), ((4, HEADS, ROWS), f32),
               ((D, LANES), bf), ((D, LANES), bf), ((LANES, D), bf), ((LANES, D), bf), ((T, LANES), f32), ((T, LANES), bf),
               ((T, D), f32), ((T, D), f32), ((D, LANES), f32), ((4, ROWS, LANES), bf), ((4, 8, ROWS, 2 * D), bf),
               ((8, 4, ROWS, 2 * D), bf), ((4, ROWS, 2 * D), f32)]
    return pl.pallas_call(
        kernel,
        out_shape=[jax.ShapeDtypeStruct(s, bf) for s in (
            (1, ROWS, 4 * LANES), (1, ROWS, 4 * D), (1, ROWS, 4 * D), (4, ROWS, XCOLS), (4, ROWS, 4 * D))],
        in_specs=[anyspace] * 6, out_specs=[anyspace] * 5,
        scratch_shapes=[pltpu.VMEM(*s) for s in scratch] + [dma(s) for s in shapes],
        compiler_params=pltpu.CompilerParams(vmem_limit_bytes=60 << 20, collective_id=0, has_side_effects=True),
        name="attention_backward")(q, g, o, k, v, xin)


def per_device(x_in, q, k, v, o, g):
    dq, dk, dv, xr, dvall = whole(q, g, o, k, v, x_in)
    w = dot(xr.reshape(4 * ROWS, XCOLS), dvall.reshape(4 * ROWS, 4 * D), 0, 0).astype(bf)
    w = lax.all_to_all(w.reshape(64, -1, 4 * D), ("z", "y", "h", "c"), 0, 0, tiled=True)
    return dq, dk, dv, w.astype(f32).sum(axis=0)


def solution(mesh):
    fine = Mesh(mesh.devices.reshape(4, 2, 4, 4, 2), ("x", "z", "y", "h", "c"))
    seq, dp = ("x", "z", "y"), ("h", "c")
    rows = P(dp, seq, None)
    return jax.shard_map(per_device, mesh=fine, in_specs=(rows,) * 6,
                         out_specs=(rows, rows, rows, P(seq + dp, None)), check_vma=False)
```

```python
import jax
import jax.numpy as jnp
from jax import lax
from jax.sharding import Mesh, PartitionSpec as P
from jax.experimental import pallas as pl
from jax.experimental.pallas import tpu as pltpu

bf = jnp.bfloat16
f32 = jnp.float32
HEADS = 8
D = 128
ROWS = 128
LANES = HEADS * ROWS
SCALE = D ** -0.5
LOG = SCALE * 1.4426950408889634
CHUNK = 512
BLOCKS = CHUNK // ROWS
XCOLS = 1280


def dot(a, b, ca, cb):
    return lax.dot_general(a, b, (((ca,), (cb,)), ((), ())), preferred_element_type=f32)


def cols(index, width):
    return pl.ds(pl.multiple_of(index * width, width), width)


def remote(src, dst, sems, at, peer, there=None):
    return pltpu.make_async_remote_copy(src_ref=src, dst_ref=dst, send_sem=sems[0].at[at],
                                        recv_sem=sems[1].at[at if there is None else there],
                                        device_id=peer, device_id_type=pl.DeviceIdType.MESH)


def arrived(ref, sem):
    pltpu.make_async_copy(ref, ref, sem).wait()


def kernel(q, g, o, k, v, xin, dqo, dko, dvo, wo,
           kv, kt, qr, gr, dr, gl, xl, dl, qt, gt, qn, gn, rs, sh, S, E, dka, dva, dqt, dqv, part, rcv, fin,
           xp, xr, xt, dvall, wb, wrc, w2, wrp, w3, wrh, *sems):
    (lg, lo), sk, sv, sq, sg, sd, sx, sb, sc, sdq, sp, srk, srv, sdv, swc, swp, swh = [
        sems[i:i + 2] for i in range(0, 34, 2)]
    x, z, y, h, c = (lax.axis_index(a) for a in ("x", "z", "y", "h", "c"))
    me = 8 * x + 4 * z + y

    def mod4(i):
        return lax.rem(i + 4, 4)

    xs = [mod4(x + d) for d in range(4)]
    ys = [mod4(y + e) for e in range(4)]
    hs = [mod4(h + e) for e in range(4)]
    near = [(dz, e) for dz in range(2) for e in range(4) if dz or e]

    def in_plane(dz, e):
        return {"z": (1 - z) if dz else z, "y": ys[e]}

    def in_side(dz, d):
        return {"x": xs[d], "z": (1 - z) if dz else z}

    barrier = pltpu.get_barrier_semaphore()
    friends = [{"x": xs[d], "y": ys[e]} for d in range(4) for e in range(4) if d or e]
    friends += [in_plane(1, e) for e in range(4)] + [in_side(1, d) for d in (1, 2, 3)]
    friends += [{"c": 1 - c}] + [{"h": hs[e]} for e in (1, 2, 3)]
    for friend in friends:
        pl.semaphore_signal(barrier, inc=1, device_id=friend, device_id_type=pl.DeviceIdType.MESH)
    get_g = pltpu.make_async_copy(g.at[0], gl, lg)
    get_o = pltpu.make_async_copy(o.at[0], xl.at[:, 0:4 * LANES], lo)
    get_x = pltpu.make_async_copy(xin.at[0], xl, lo)
    get_g.start()
    get_o.start()
    pl.semaphore_wait(barrier, len(friends))

    sends = []

    def send(*a):
        copy = remote(*a)
        copy.start()
        sends.append(copy)

    for src, dst, s, width in ((k.at[0], kv.at[me, :, 0:D], sk, D), (v.at[0], kv.at[me, :, D:2 * D], sv, D),
                               (q.at[0], qr.at[x], sq, LANES), (g.at[0], gr.at[x], sg, LANES)):
        for d in (1, 3, 2):
            send(src.at[:, cols(xs[d], width)], dst, s, d, {"x": xs[d]})
        pltpu.make_async_copy(src.at[:, cols(x, width)], dst, s[1].at[0]).start()

    get_g.wait()
    get_o.wait()
    head = lax.broadcasted_iota(jnp.int32, (HEADS, LANES), 0)
    ones = jnp.where(head == lax.broadcasted_iota(jnp.int32, (HEADS, LANES), 1) // D, 1.0, 0.0).astype(bf)
    for j in range(4):
        at = slice(j * LANES, (j + 1) * LANES)
        prod = gl[:, at].astype(f32) * xl[:, at].astype(f32)
        high = prod.astype(bf)
        low = (prod - high.astype(f32)).astype(bf)
        dl[j] = dot(ones, high, 1, 1) + dot(ones, low, 1, 1)
    get_x.start()
    for d in (1, 3, 2):
        send(dl.at[xs[d]], dr.at[x], sd, d, {"x": xs[d]})
    pltpu.make_async_copy(dl.at[x], dr.at[x], sd[1].at[0]).start()

    def slot(s, zz, yy):
        return kv.at[8 * s + 4 * zz + yy]

    for s in range(4):
        d = mod4(x - s)
        mine = slot(s, z, y)
        arrived(mine.at[:, 0:D], sk[1].at[d])
        arrived(mine.at[:, D:2 * D], sv[1].at[d])
        for e in (1, 3, 2):
            send(mine, mine, sc, (s, e), {"y": ys[e]})
        send(mine, mine, sb, (s, 0), {"z": 1 - z})

    get_x.wait()
    for j in range(4):
        xp[j] = jnp.concatenate([xl[:, 640 * b + 160 * j:640 * b + 160 * j + 160] for b in range(8)], axis=1)
    for e in (1, 3, 2):
        send(xp.at[ys[e]], xr.at[y], sx, e, {"y": ys[e]})
    pltpu.make_async_copy(xp.at[y], xr.at[y], sx[1].at[0]).start()

    dka[...] = jnp.zeros_like(dka)
    dva[...] = jnp.zeros_like(dva)
    dqt[...] = jnp.zeros_like(dqt)

    def relay(s):
        for e in (1, 3, 2):
            theirs = slot(s, z, mod4(y - e))
            arrived(theirs, sc[1].at[s, e])
            remote(theirs, theirs, sb, (s, e), {"z": 1 - z}).start()

    def chunk_of(ch):
        return pl.ds(ch * BLOCKS, BLOCKS)

    def stats(s, carry):
        d = mod4(x - s)
        i = 8 * s + 4 * z + y
        for e in range(4):
            arrived(slot(s, 1 - z, mod4(y - e)), sb[1].at[s, e])
        for b in range(8):
            kt[:, cols(8 * s + b, D)] = kv[8 * s + b, :, 0:D].T
        arrived(qr.at[s], sq[1].at[d])
        arrived(dr.at[s], sd[1].at[d])
        for n in range(HEADS):
            cs = slice(n * D, (n + 1) * D)
            qh = qr[s, :, cs]
            qt[:, cs] = qh.T
            qn[s, cs, :] = qh
        n = i // BLOCKS

        def score(ch):
            return dot(kv[chunk_of(ch), :, 0:D].reshape(CHUNK, D), qt[...], 1, 0)

        def top(m, t):
            return jnp.maximum(m, jnp.max(t.reshape(CHUNK // 8, 8, LANES), axis=0))

        def p1(ch, m):
            t = score(ch)
            S[cols(ch, CHUNK), :] = t
            return top(m, t)

        m = lax.fori_loop(0, n, p1, jnp.full((8, LANES), -1e30, f32))
        last = score(n)
        key = n * CHUNK + lax.broadcasted_iota(jnp.int32, (CHUNK, LANES), 0)
        row = i * ROWS + lax.broadcasted_iota(jnp.int32, (CHUNK, LANES), 1) % ROWS
        last = jnp.where(key <= row, last, -1e30)
        S[cols(n, CHUNK), :] = last
        mc = jnp.max(top(m, last), axis=0, keepdims=True) * LOG

        def p2(ch, total, keep):
            e = jnp.exp2(S[cols(ch, CHUNK), :] * LOG - mc)
            if keep:
                S[cols(ch, CHUNK), :] = e
            else:
                E[cols(s * (s + 1) + ch, CHUNK), :] = e.astype(bf)
            return total + jnp.sum(e.reshape(CHUNK // 8, 8, LANES), axis=0)

        def finish(keep):
            total = lax.fori_loop(0, n + 1, lambda ch, t: p2(ch, t, keep), jnp.zeros((8, LANES), f32))
            r = 1.0 / jnp.sum(total, axis=0, keepdims=True)
            rs[s] = r
            sh[s] = jnp.concatenate([dr[s, a:a + 1, :] for a in range(HEADS)], axis=1) * r

        pl.when(s < 3)(lambda: finish(False))
        pl.when(s == 3)(lambda: finish(True))

        @pl.when(s < 2)
        def _():
            relay(s + 2)

        return carry

    relay(0)
    relay(1)
    lax.fori_loop(0, 4, stats, 0)

    def scale(s, carry):
        arrived(gr.at[s], sg[1].at[mod4(x - s)])
        for n in range(HEADS):
            cs = slice(n * D, (n + 1) * D)
            gh = (gr[s, :, cs].astype(f32).T * rs[s, :, cs]).astype(bf)
            gt[s, :, cs] = gh
            gn[s, cs, :] = gh.T
        return carry

    lax.fori_loop(0, 4, scale, 0)

    def grads(s, ch, e32, e):
        at = cols(ch, CHUNK)
        values = kv[chunk_of(ch), :, D:2 * D].reshape(CHUNK, D)
        ds = (e32 * (dot(values, gt[s], 1, 0) - sh[s])).astype(bf)
        dva[at, :] += dot(e, gn[s], 1, 0)
        dka[at, :] += dot(ds, qn[s], 1, 0)
        dqt[s] += dot(kt[:, at], ds, 1, 0)

    def wide(ch, carry):
        e = S[cols(ch, CHUNK), :]
        grads(3, ch, e, e.astype(bf))
        return carry

    def reduce(s):
        own = 4 * z + y
        total = part[s, own].astype(f32)
        for dz, e in near:
            n = dz * 4 + e
            arrived(rcv.at[n, s], sp[1].at[n, s])
            total = total + rcv[n, s].astype(f32)
        fin[s] = total.astype(bf)

        def deliver(src, dst, s2, at, there, peer, local):
            @pl.when(local)
            def _():
                pltpu.make_async_copy(src, dst, s2[1].at[there]).start()

            @pl.when(jnp.logical_not(local))
            def _():
                remote(src, dst, s2, at, peer, there).start()

        home = s == x
        for e in range(4):
            if e:
                remote(fin.at[s, :, D:2 * D], dvall.at[y, :, cols(x, D)], sdv, (s, e), {"x": s, "y": ys[e]}, (x, y)).start()
            else:
                deliver(fin.at[s, :, D:2 * D], dvall.at[y, :, cols(x, D)], sdv, (s, 0), (x, y), {"x": s}, home)
        deliver(fin.at[s, :, 0:D], dko.at[0, :, cols(x, D)], srk, s, x, {"x": s}, home)
        deliver(fin.at[s, :, D:2 * D], dvo.at[0, :, cols(x, D)], srv, s, x, {"x": s}, home)

    def group(turn, carry):
        a = 3 - turn
        lax.fori_loop(2 * a, jnp.minimum(2 * a + 2, 7 + z), wide, 0)

        def narrow(s, carry):
            def one(ch, carry):
                e = E[cols(s * (s + 1) + ch, CHUNK), :]
                grads(s, ch, e.astype(f32), e)
                return carry

            lax.fori_loop(2 * a, jnp.minimum(2 * a + 2, 2 * s + 1 + z), one, 0)
            return carry

        lax.fori_loop(a, 3, narrow, 0)
        for b in range(8):
            at = pl.ds(pl.multiple_of(a * 1024 + b * ROWS, ROWS), ROWS)
            part[a, b, :, 0:D] = (dka[at, :] * SCALE).astype(bf)
            part[a, b, :, D:2 * D] = dva[at, :].astype(bf)
        for dz, e in near:
            peer = in_plane(dz, e)
            n = dz * 4 + e
            remote(part.at[a, 4 * peer["z"] + peer["y"]], rcv.at[n, a], sp, (n, a), peer).start()

        @pl.when(turn > 0)
        def _():
            reduce(a + 1)

        @pl.when(turn == 1)
        def _():
            line = lax.broadcasted_iota(jnp.int32, (320, 640), 0)
            want = line + 20 * lax.shift_right_logical(line * 3277, 16)
            place = lax.broadcasted_iota(jnp.int32, (320, 640), 1)
            for e in range(4):
                arrived(xr.at[mod4(y - e)], sx[1].at[e])
            for part_c in range(2):
                pick = jnp.where(place == want + 20 * part_c, 1.0, 0.0).astype(bf)
                for half in range(2):
                    for j in range(4):
                        xt[part_c, half * 320:half * 320 + 320, j * ROWS:(j + 1) * ROWS] = dot(
                            pick, xr[j, :, half * 640:half * 640 + 640], 1, 1).astype(bf)

        return carry

    lax.fori_loop(0, 4, group, 0)

    def give_dq(t, carry):
        s = 3 - t
        for n in range(HEADS):
            cs = slice(n * D, (n + 1) * D)
            dqv[s, :, cs] = (dqt[s, :, cs].T * SCALE).astype(bf)
        home = dqo.at[0, :, cols(x, LANES)]

        @pl.when(s == x)
        def _():
            pltpu.make_async_copy(dqv.at[s], home, sdq[1].at[0]).start()

        @pl.when(s != x)
        def _():
            remote(dqv.at[s], home, sdq, mod4(s - x), {"x": s}).start()

        return carry

    lax.fori_loop(0, 4, give_dq, 0)
    reduce(0)

    for j in range(4):
        for b in range(4):
            arrived(dvall.at[b, :, cols(j, D)], sdv[1].at[j, b])
    tall = dvall[...].reshape(4 * ROWS, 4 * D)

    def weigh(part_c):
        for t in range(4):
            at = slice(t * 160, t * 160 + 160)
            wb[part_c, at, :] = dot(xt[part_c, at, :], tall, 1, 0).astype(bf)

    weigh(1 - c)
    send(wb.at[1 - c], wrc, swc, 0, {"c": 1 - c})
    weigh(c)
    arrived(wrc, swc[1].at[0])
    for b in range(8):
        at = slice(b * 80, b * 80 + 80)
        w2[b] = (wb[c, at, :].astype(f32) + wrc[at, :].astype(f32)).astype(bf)
    for dz, d in near:
        peer = in_side(dz, d)
        send(w2.at[2 * peer["x"] + peer["z"]], wrp.at[dz * 4 + d], swp, dz * 4 + d, peer)
    total = w2[2 * x + z].astype(f32)
    for dz, d in near:
        n = dz * 4 + d
        arrived(wrp.at[n], swp[1].at[n])
        total = total + wrp[n].astype(f32)
    for e in range(4):
        w3[e] = jnp.concatenate([total[20 * e:20 * e + 20], jnp.zeros((12, 4 * D), f32)], axis=0).astype(bf)
    for e in (1, 3, 2):
        send(w3.at[hs[e]], wrh.at[e], swh, e, {"h": hs[e]})
    last = w3[h].astype(f32)
    for e in (1, 3, 2):
        arrived(wrh.at[e], swh[1].at[e])
        last = last + wrh[e].astype(f32)
    wo[...] = last[0:20]

    for d in range(4):
        f = mod4(x - d)
        arrived(dqo.at[0, :, cols(f, LANES)], sdq[1].at[d])
        arrived(dko.at[0, :, cols(d, D)], srk[1].at[d])
        arrived(dvo.at[0, :, cols(d, D)], srv[1].at[d])
    for copy in sends:
        copy.wait_send()
    for s in range(4):
        for e in (1, 2, 3):
            theirs = slot(s, z, mod4(y - e))
            remote(theirs, theirs, sb, (s, e), {"z": 1 - z}).wait_send()
    for d in (1, 2, 3):
        remote(dqv.at[xs[d]], dqo.at[0, :, cols(x, LANES)], sdq, d, {"x": xs[d]}).wait_send()
    for dz, e in near:
        n = dz * 4 + e
        for a in range(4):
            remote(part.at[a, 0], rcv.at[n, a], sp, (n, a), in_plane(dz, e)).wait_send()
    for s in range(4):
        for e in (1, 2, 3):
            remote(fin.at[s, :, D:2 * D], dvall.at[y, :, cols(x, D)], sdv, (s, e), {"y": ys[e]}).wait_send()
    for d in (1, 2, 3):
        t = xs[d]
        remote(fin.at[t, :, D:2 * D], dvall.at[y, :, cols(x, D)], sdv, (t, 0), {"x": t}).wait_send()
        remote(fin.at[t, :, 0:D], dko.at[0, :, cols(x, D)], srk, t, {"x": t}).wait_send()
        remote(fin.at[t, :, D:2 * D], dvo.at[0, :, cols(x, D)], srv, t, {"x": t}).wait_send()


def per_device(x_in, q, k, v, o, g):
    T = 32 * ROWS
    anyspace = pl.BlockSpec(memory_space=pl.ANY)
    sems = [(), ()] + [(4,)] * 12 + [(4, 4)] * 4 + [(4,)] * 2 + [(8, 4)] * 2 + [(4,)] * 4 + [(4, 4)] * 2 + [(1,)] * 2
    sems += [(8,)] * 2 + [(4,)] * 2
    wide, tall = (ROWS, 4 * LANES), (T, D)
    scratch = [((32, ROWS, 2 * D), bf), ((D, T), bf), ((4, ROWS, LANES), bf), ((4, ROWS, LANES), bf), ((4, HEADS, ROWS), f32),
               (wide, bf), ((ROWS, 4 * XCOLS), bf), ((4, HEADS, ROWS), f32), ((D, LANES), bf), ((4, D, LANES), bf),
               ((4, LANES, D), bf), ((4, LANES, D), bf), ((4, 1, LANES), f32), ((4, 1, LANES), f32),
               ((T, LANES), f32), ((12 * CHUNK, LANES), bf), (tall, f32), (tall, f32), ((4, D, LANES), f32),
               ((4, ROWS, LANES), bf), ((4, 8, ROWS, 2 * D), bf), ((8, 4, ROWS, 2 * D), bf), ((4, ROWS, 2 * D), bf),
               ((4, ROWS, XCOLS), bf), ((4, ROWS, XCOLS), bf), ((2, XCOLS // 2, 4 * ROWS), bf), ((4, ROWS, 4 * D), bf),
               ((2, XCOLS // 2, 4 * D), bf), ((XCOLS // 2, 4 * D), bf), ((8, 80, 4 * D), bf), ((8, 80, 4 * D), bf),
               ((4, 32, 4 * D), bf), ((4, 32, 4 * D), bf)]
    return pl.pallas_call(
        kernel,
        out_shape=[jax.ShapeDtypeStruct((1, ROWS, 4 * LANES), bf), jax.ShapeDtypeStruct((1, ROWS, 4 * D), bf),
                   jax.ShapeDtypeStruct((1, ROWS, 4 * D), bf), jax.ShapeDtypeStruct((20, 4 * D), f32)],
        in_specs=[anyspace] * 6,
        out_specs=[anyspace] * 3 + [pl.BlockSpec(memory_space=pltpu.VMEM)],
        scratch_shapes=[pltpu.VMEM(*s) for s in scratch] + [pltpu.SemaphoreType.DMA(s) for s in sems],
        compiler_params=pltpu.CompilerParams(vmem_limit_bytes=62 << 20, collective_id=0, has_side_effects=True),
        name="attention_backward")(q, g, o, k, v, x_in)


def solution(mesh):
    fine = Mesh(mesh.devices.reshape(4, 2, 4, 4, 2), ("x", "z", "y", "h", "c"))
    seq, dp = ("x", "z", "y"), ("h", "c")
    rows = P(dp, seq, None)
    return jax.shard_map(per_device, mesh=fine, in_specs=(rows,) * 6,
                         out_specs=(rows, rows, rows, P(seq + dp, None)), check_vma=False)
```

```python
import jax
import jax.numpy as jnp
from jax import lax
from jax.sharding import Mesh, PartitionSpec as P
from jax.experimental import pallas as pl
from jax.experimental.pallas import tpu as pltpu

bf = jnp.bfloat16
f32 = jnp.float32
HEADS = 8
D = 128
ROWS = 128
LANES = HEADS * ROWS
SCALE = D ** -0.5
LOG = SCALE * 1.4426950408889634
CHUNK = 512
BLOCKS = CHUNK // ROWS
XCOLS = 1280


def dot(a, b, ca, cb):
    return lax.dot_general(a, b, (((ca,), (cb,)), ((), ())), preferred_element_type=f32)


def cols(index, width):
    return pl.ds(pl.multiple_of(index * width, width), width)


def remote(src, dst, sems, at, peer, there=None):
    return pltpu.make_async_remote_copy(src_ref=src, dst_ref=dst, send_sem=sems[0].at[at],
                                        recv_sem=sems[1].at[at if there is None else there],
                                        device_id=peer, device_id_type=pl.DeviceIdType.MESH)


def arrived(ref, sem):
    pltpu.make_async_copy(ref, ref, sem).wait()


def kernel(q, g, o, k, v, xin, dqo, dko, dvo, wo,
           kv, kt, qr, gr, dr, gl, xl, dl, qn, gn, rs, sh, S, E, dka, dva, dqt, dqv, partk, partv, rcvk, rcvv, fink, finv,
           xp, xr, xt, dvall, wb, wrc, w2, wrp, w3, wrh, *sems):
    (lg, lo), sk, sv, sq, sg, sd, sx, sb, sc, sc2, sdq, spk, spv, srk, srv, sdv, swc, swp, swh = [
        sems[i:i + 2] for i in range(0, 38, 2)]
    x, z, y, h, c = (lax.axis_index(a) for a in ("x", "z", "y", "h", "c"))
    me = 8 * x + 4 * z + y

    def mod4(i):
        return lax.rem(i + 4, 4)

    xs = [mod4(x + d) for d in range(4)]
    ys = [mod4(y + e) for e in range(4)]
    hs = [mod4(h + e) for e in range(4)]
    near = [(dz, e) for dz in range(2) for e in range(4) if dz or e]

    def in_plane(dz, e):
        return {"z": (1 - z) if dz else z, "y": ys[e]}

    def in_side(dz, d):
        return {"x": xs[d], "z": (1 - z) if dz else z}

    barrier = pltpu.get_barrier_semaphore()
    friends = [{"x": xs[d], "y": ys[e]} for d in range(4) for e in range(4) if d or e]
    friends += [in_plane(1, e) for e in range(4)] + [in_side(1, d) for d in (1, 2, 3)]
    friends += [{"c": 1 - c}] + [{"h": hs[e]} for e in (1, 2, 3)]
    for friend in friends:
        pl.semaphore_signal(barrier, inc=1, device_id=friend, device_id_type=pl.DeviceIdType.MESH)
    get_g = pltpu.make_async_copy(g.at[0], gl, lg)
    get_o = pltpu.make_async_copy(o.at[0], xl.at[:, 0:4 * LANES], lo)
    get_x = pltpu.make_async_copy(xin.at[0], xl, lo)
    get_g.start()
    get_o.start()
    pl.semaphore_wait(barrier, len(friends))

    sends = []

    def send(*a):
        copy = remote(*a)
        copy.start()
        sends.append(copy)

    def spread(src, dst, s, width, which):
        for d in which:
            send(src.at[0, :, cols(xs[d], width)], dst, s, d, {"x": xs[d]})

    def stay(src, dst, s, width):
        pltpu.make_async_copy(src.at[0, :, cols(x, width)], dst, s[1].at[0]).start()

    spread(k, kv.at[me, :, 0:D], sk, D, (1, 3, 2))
    spread(v, kv.at[me, :, D:2 * D], sv, D, (1, 3, 2))
    stay(k, kv.at[me, :, 0:D], sk, D)
    stay(v, kv.at[me, :, D:2 * D], sv, D)
    spread(q, qr.at[x], sq, LANES, (1, 3))
    stay(q, qr.at[x], sq, LANES)
    stay(g, gr.at[x], sg, LANES)

    get_g.wait()
    get_o.wait()
    head = lax.broadcasted_iota(jnp.int32, (HEADS, LANES), 0)
    ones = jnp.where(head == lax.broadcasted_iota(jnp.int32, (HEADS, LANES), 1) // D, 1.0, 0.0).astype(bf)
    for j in range(4):
        at = slice(j * LANES, (j + 1) * LANES)
        prod = gl[:, at].astype(f32) * xl[:, at].astype(f32)
        high = prod.astype(bf)
        low = (prod - high.astype(f32)).astype(bf)
        dl[j] = dot(ones, high, 1, 1) + dot(ones, low, 1, 1)
    get_x.start()
    for d in (1, 3, 2):
        send(dl.at[xs[d]], dr.at[x], sd, d, {"x": xs[d]})
    pltpu.make_async_copy(dl.at[x], dr.at[x], sd[1].at[0]).start()

    def slot(s, zz, yy):
        return kv.at[8 * s + 4 * zz + yy]

    for s in range(4):
        d = mod4(x - s)
        mine = slot(s, z, y)
        arrived(mine.at[:, 0:D], sk[1].at[d])
        arrived(mine.at[:, D:2 * D], sv[1].at[d])
        send(mine, mine, sb, (s, 0), {"z": 1 - z})
        for e in (1, 3, 2):
            send(mine, mine, sc, (s, e), {"y": ys[e]})

    spread(q, qr.at[x], sq, LANES, (2,))
    spread(g, gr.at[x], sg, LANES, (1, 3))

    get_x.wait()
    for j in range(4):
        xp[j] = jnp.concatenate([xl[:, 640 * b + 160 * j:640 * b + 160 * j + 160] for b in range(8)], axis=1)
    dka[...] = jnp.zeros_like(dka)
    dqt[...] = jnp.zeros_like(dqt)

    for s in (0, 1):
        theirs = slot(s + 2, 1 - z, y)
        arrived(theirs, sb[1].at[s + 2, 0])
        for e in (1, 3, 2):
            send(theirs, theirs, sc2, (s + 2, e), {"y": ys[e]})
        for e in (1, 3, 2):
            theirs = slot(s, z, mod4(y - e))
            arrived(theirs, sc[1].at[s, e])
            send(theirs, theirs, sb, (s, e), {"z": 1 - z})
    spread(g, gr.at[x], sg, LANES, (2,))
    for e in (1, 3, 2):
        send(xp.at[ys[e]], xr.at[y], sx, e, {"y": ys[e]})
    pltpu.make_async_copy(xp.at[y], xr.at[y], sx[1].at[0]).start()

    def chunk_of(ch):
        return pl.ds(ch * BLOCKS, BLOCKS)

    def stats(s, carry):
        d = mod4(x - s)
        i = 8 * s + 4 * z + y

        @pl.when(s < 2)
        def _():
            for e in range(4):
                arrived(slot(s, 1 - z, mod4(y - e)), sb[1].at[s, e])

        @pl.when(s >= 2)
        def _():
            for e in (1, 2, 3):
                arrived(slot(s, z, mod4(y - e)), sc[1].at[s, e])
                arrived(slot(s, 1 - z, mod4(y - e)), sc2[1].at[s, e])

        for b in range(8):
            kt[:, cols(8 * s + b, D)] = kv[8 * s + b, :, 0:D].T
        arrived(qr.at[s], sq[1].at[d])
        arrived(dr.at[s], sd[1].at[d])
        for n in range(HEADS):
            cs = slice(n * D, (n + 1) * D)
            qn[s, cs, :] = qr[s, :, cs]
        n = i // BLOCKS

        def score(ch):
            return dot(kv[chunk_of(ch), :, 0:D].reshape(CHUNK, D), qn[s], 1, 1)

        def top(m, t):
            return jnp.maximum(m, jnp.max(t.reshape(CHUNK // 8, 8, LANES), axis=0))

        def p1(ch, m):
            t = score(ch)
            S[cols(ch, CHUNK), :] = t
            return top(m, t)

        m = lax.fori_loop(0, n, p1, jnp.full((8, LANES), -1e30, f32))
        last = score(n)
        key = n * CHUNK + lax.broadcasted_iota(jnp.int32, (CHUNK, LANES), 0)
        row = i * ROWS + lax.broadcasted_iota(jnp.int32, (CHUNK, LANES), 1) % ROWS
        last = jnp.where(key <= row, last, -1e30)
        S[cols(n, CHUNK), :] = last
        mc = jnp.max(top(m, last), axis=0, keepdims=True) * LOG

        def p2(ch, total, keep):
            e = jnp.exp2(S[cols(ch, CHUNK), :] * LOG - mc)
            if keep:
                S[cols(ch, CHUNK), :] = e
            else:
                E[cols(s * (s + 1) + ch, CHUNK), :] = e.astype(bf)
            return total + jnp.sum(e.reshape(CHUNK // 8, 8, LANES), axis=0)

        def finish(keep):
            total = lax.fori_loop(0, n + 1, lambda ch, t: p2(ch, t, keep), jnp.zeros((8, LANES), f32))
            r = 1.0 / jnp.sum(total, axis=0, keepdims=True)
            rs[s] = r
            sh[s] = jnp.concatenate([dr[s, a:a + 1, :] for a in range(HEADS)], axis=1) * r

        pl.when(s < 3)(lambda: finish(False))
        pl.when(s == 3)(lambda: finish(True))

        return carry

    lax.fori_loop(0, 4, stats, 0)

    def scale(s, carry):
        arrived(gr.at[s], sg[1].at[mod4(x - s)])
        heads = jnp.concatenate([rs[s, :, n * D:(n + 1) * D] for n in range(HEADS)], axis=0).T
        for n in range(HEADS):
            cs = slice(n * D, (n + 1) * D)
            gn[s, cs, :] = (gr[s, :, cs].astype(f32) * heads[:, n:n + 1]).astype(bf)
        return carry

    def grads(s, ch, e32):
        at = cols(ch, CHUNK)
        values = kv[chunk_of(ch), :, D:2 * D].reshape(CHUNK, D)
        ds = (e32 * (dot(values, gn[s], 1, 1) - sh[s])).astype(bf)
        dka[at, :] += dot(ds, qn[s], 1, 0)
        dqt[s] += dot(kt[:, at], ds, 1, 0)

    def wide(ch, carry):
        grads(3, ch, S[cols(ch, CHUNK), :])
        return carry

    def narrow(s, first, end):
        def one(ch, carry):
            grads(s, ch, E[cols(s * (s + 1) + ch, CHUNK), :].astype(f32))
            return carry

        lax.fori_loop(first, end, one, 0)

    def give_dq(s):
        for n in range(HEADS):
            cs = slice(n * D, (n + 1) * D)
            dqv[s, :, cs] = (dqt[s, :, cs] * SCALE).astype(bf).T
        home = dqo.at[0, :, cols(x, LANES)]

        @pl.when(s == x)
        def _():
            pltpu.make_async_copy(dqv.at[s], home, sdq[1].at[0]).start()

        @pl.when(s != x)
        def _():
            remote(dqv.at[s], home, sdq, mod4(s - x), {"x": s}).start()

    def total_of(part, rcv, sems, s):
        total = part[s, 4 * z + y].astype(f32)
        for dz, e in near:
            n = dz * 4 + e
            arrived(rcv.at[n, s], sems[1].at[n, s])
            total = total + rcv[n, s].astype(f32)
        return total.astype(bf)

    def deliver(src, dst, s2, at, there, s):
        @pl.when(s == x)
        def _():
            pltpu.make_async_copy(src, dst, s2[1].at[there]).start()

        @pl.when(s != x)
        def _():
            remote(src, dst, s2, at, {"x": s}, there).start()

    def reduce_v(s, carry):
        finv[s] = total_of(partv, rcvv, spv, s)
        place = dvall.at[y, :, cols(x, D)]
        for e in (1, 3, 2):
            remote(finv.at[s], place, sdv, (s, e), {"x": s, "y": ys[e]}, (x, y)).start()
        deliver(finv.at[s], place, sdv, (s, 0), (x, y), s)
        deliver(finv.at[s], dvo.at[0, :, cols(x, D)], srv, s, x, s)
        return carry

    def reduce_k(s):
        fink[s] = total_of(partk, rcvk, spk, s)
        deliver(fink.at[s], dko.at[0, :, cols(x, D)], srk, s, x, s)

    def hand_out(part, rcv, sems, a, zz):
        dz = lax.rem(z + zz, 2)
        for e in range(4):
            n = dz * 4 + e

            @pl.when(n > 0)
            def _():
                remote(part.at[a, 4 * zz + ys[e]], rcv.at[n, a], sems, (n, a), {"z": zz, "y": ys[e]}).start()

    def values_of(a):
        def one(i, carry):
            zz = 1 - i
            ch = 2 * a + zz

            def share(s):
                e = S[cols(ch, CHUNK), :].astype(bf) if s == 3 else E[cols(s * (s + 1) + ch, CHUNK), :]
                return dot(e, gn[s], 1, 0)

            dva[...] = sum([share(s) for s in range(a + 1, 4)], jnp.zeros((CHUNK, D), f32))

            @pl.when(zz <= z)
            def _():
                dva[...] += share(a)

            for b in range(4):
                partv[a, 4 * zz + b] = dva[b * ROWS:(b + 1) * ROWS, :].astype(bf)
            hand_out(partv, rcvv, spv, a, zz)
            return carry

        lax.fori_loop(0, 2, one, 0)

    order = [(1, 2), (1, 1), (1, 3), (0, 2), (0, 1), (0, 3), (1, 0), (0, 0)]

    def piece(dz, d):
        peer = in_side(dz, d)
        return peer, 2 * peer["x"] + peer["z"]

    def turn_x():
        line = lax.broadcasted_iota(jnp.int32, (320, 640), 0)
        want = line + 20 * lax.shift_right_logical(line * 3277, 16)
        place = lax.broadcasted_iota(jnp.int32, (320, 640), 1)
        for e in range(4):
            arrived(xr.at[mod4(y - e)], sx[1].at[e])
        for part_c in range(2):
            pick = jnp.where(place == want + 20 * part_c, 1.0, 0.0).astype(bf)
            for half in range(2):
                for j in range(4):
                    rows = dot(pick, xr[j, :, half * 640:half * 640 + 640], 1, 1).astype(bf)
                    xt[part_c, half * 4:half * 4 + 4, :, j * ROWS:(j + 1) * ROWS] = rows.reshape(4, 80, ROWS)


    def weigh():
        for j in range(4):
            for b in range(4):
                arrived(dvall.at[b, :, cols(j, D)], sdv[1].at[j, b])
        tall = dvall[...].reshape(4 * ROWS, 4 * D)

        def product(half):
            wb[half] = dot(xt[half].reshape(640, 4 * ROWS), tall, 1, 0).astype(bf).reshape(8, 80, 4 * D)

        product(1 - c)
        for n, (dz, d) in enumerate(order):
            b = piece(dz, d)[1]
            remote(wb.at[1 - c, b], wrc.at[b], swc, n, {"c": 1 - c}).start()
        product(c)

    def over_sides():
        for n, (dz, d) in enumerate(order):
            peer, b = piece(dz, d)
            arrived(wrc.at[b], swc[1].at[n])
            w2[b] = (wb[c, b].astype(f32) + wrc[b].astype(f32)).astype(bf)
            if dz or d:
                remote(w2.at[b], wrp.at[dz * 4 + d], swp, dz * 4 + d, peer).start()

    def over_rest():
        total = w2[2 * x + z].astype(f32)
        for dz, d in near:
            n = dz * 4 + d
            arrived(wrp.at[n], swp[1].at[n])
            total = total + wrp[n].astype(f32)
        for e in range(4):
            w3[e] = jnp.concatenate([total[20 * e:20 * e + 20], jnp.zeros((12, 4 * D), f32)], axis=0).astype(bf)
        for e in (1, 3, 2):
            remote(w3.at[hs[e]], wrh.at[e], swh, e, {"h": hs[e]}).start()

    def step(t, carry):
        ch = 7 - t
        a = ch // 2
        zz = ch - 2 * a
        lax.fori_loop(ch, jnp.minimum(ch + 1, 7 + z), wide, 0)

        narrow(2, ch, jnp.minimum(ch + 1, 5 + z))
        for b in range(4):
            at = pl.ds(pl.multiple_of(ch * CHUNK + b * ROWS, ROWS), ROWS)
            partk[a, 4 * zz + b] = (dka[at, :] * SCALE).astype(bf)
        hand_out(partk, rcvk, spk, a, zz)

        @pl.when(jnp.logical_and(t > 1, zz == z))
        def _():
            reduce_k(a + 1)

        pl.when(t == 1)(weigh)
        pl.when(t == 3)(over_sides)
        pl.when(t == 5)(over_rest)
        return carry

    lax.fori_loop(0, 4, scale, 0)
    for a in (3, 2, 1, 0):
        values_of(a)

    def early(s, carry):
        narrow(s, 0, 2 * s + 1 + z)
        give_dq(s)
        return carry

    lax.fori_loop(0, 2, early, 0)
    lax.fori_loop(0, 4, reduce_v, 0)
    turn_x()
    lax.fori_loop(0, 8, step, 0)
    lax.fori_loop(2, 4, lambda s, carry: (give_dq(s), carry)[1], 0)
    last = w3[h].astype(f32)
    for e in (1, 3, 2):
        arrived(wrh.at[e], swh[1].at[e])
        last = last + wrh[e].astype(f32)
    wo[...] = last[0:20]
    reduce_k(0)

    for d in range(4):
        f = mod4(x - d)
        arrived(dqo.at[0, :, cols(f, LANES)], sdq[1].at[d])
        arrived(dko.at[0, :, cols(d, D)], srk[1].at[d])
        arrived(dvo.at[0, :, cols(d, D)], srv[1].at[d])
    for copy in sends:
        copy.wait_send()
    for d in (1, 2, 3):
        remote(dqv.at[xs[d]], dqo.at[0, :, cols(x, LANES)], sdq, d, {"x": xs[d]}).wait_send()
    for dz, e in near:
        n = dz * 4 + e
        for a in range(4):
            remote(partk.at[a, 0], rcvk.at[n, a], spk, (n, a), in_plane(dz, e)).wait_send()
            remote(partv.at[a, 0], rcvv.at[n, a], spv, (n, a), in_plane(dz, e)).wait_send()
    for s in range(4):
        for e in (1, 2, 3):
            remote(finv.at[s], dvall.at[y, :, cols(x, D)], sdv, (s, e), {"y": ys[e]}).wait_send()
    for d in (1, 2, 3):
        t = xs[d]
        remote(finv.at[t], dvall.at[y, :, cols(x, D)], sdv, (t, 0), {"x": t}).wait_send()
        remote(fink.at[t], dko.at[0, :, cols(x, D)], srk, t, {"x": t}).wait_send()
        remote(finv.at[t], dvo.at[0, :, cols(x, D)], srv, t, {"x": t}).wait_send()
    for n, (dz, d) in enumerate(order):
        peer, b = piece(dz, d)
        remote(wb.at[1 - c, b], wrc.at[b], swc, n, {"c": 1 - c}).wait_send()
        if dz or d:
            remote(w2.at[b], wrp.at[dz * 4 + d], swp, dz * 4 + d, peer).wait_send()
    for e in (1, 2, 3):
        remote(w3.at[hs[e]], wrh.at[e], swh, e, {"h": hs[e]}).wait_send()


def per_device(x_in, q, k, v, o, g):
    T = 32 * ROWS
    anyspace = pl.BlockSpec(memory_space=pl.ANY)
    sems = [(), ()] + [(4,)] * 12 + [(4, 4)] * 6 + [(4,)] * 2 + [(8, 4)] * 4 + [(4,)] * 4 + [(4, 4)] * 2 + [(8,)] * 2
    sems += [(8,)] * 2 + [(4,)] * 2
    wide, tall = (ROWS, 4 * LANES), (T, D)
    scratch = [((32, ROWS, 2 * D), bf), ((D, T), bf), ((4, ROWS, LANES), bf), ((4, ROWS, LANES), bf), ((4, HEADS, ROWS), f32),
               (wide, bf), ((ROWS, 4 * XCOLS), bf), ((4, HEADS, ROWS), f32),
               ((4, LANES, D), bf), ((4, LANES, D), bf), ((4, 1, LANES), f32), ((4, 1, LANES), f32),
               ((T, LANES), f32), ((12 * CHUNK, LANES), bf), (tall, f32), ((CHUNK, D), f32), ((4, D, LANES), f32),
               ((4, ROWS, LANES), bf), ((4, 8, ROWS, D), bf), ((4, 8, ROWS, D), bf), ((8, 4, ROWS, D), bf),
               ((8, 4, ROWS, D), bf), ((4, ROWS, D), bf), ((4, ROWS, D), bf),
               ((4, ROWS, XCOLS), bf), ((4, ROWS, XCOLS), bf), ((2, 8, 80, 4 * ROWS), bf), ((4, ROWS, 4 * D), bf),
               ((2, 8, 80, 4 * D), bf), ((8, 80, 4 * D), bf), ((8, 80, 4 * D), bf), ((8, 80, 4 * D), bf),
               ((4, 32, 4 * D), bf), ((4, 32, 4 * D), bf)]
    return pl.pallas_call(
        kernel,
        out_shape=[jax.ShapeDtypeStruct((1, ROWS, 4 * LANES), bf), jax.ShapeDtypeStruct((1, ROWS, 4 * D), bf),
                   jax.ShapeDtypeStruct((1, ROWS, 4 * D), bf), jax.ShapeDtypeStruct((20, 4 * D), f32)],
        in_specs=[anyspace] * 6,
        out_specs=[anyspace] * 3 + [pl.BlockSpec(memory_space=pltpu.VMEM)],
        scratch_shapes=[pltpu.VMEM(*s) for s in scratch] + [pltpu.SemaphoreType.DMA(s) for s in sems],
        compiler_params=pltpu.CompilerParams(vmem_limit_bytes=62 << 20, collective_id=0, has_side_effects=True),
        name="attention_backward")(q, g, o, k, v, x_in)


def solution(mesh):
    fine = Mesh(mesh.devices.reshape(4, 2, 4, 4, 2), ("x", "z", "y", "h", "c"))
    seq, dp = ("x", "z", "y"), ("h", "c")
    rows = P(dp, seq, None)
    return jax.shard_map(per_device, mesh=fine, in_specs=(rows,) * 6,
                         out_specs=(rows, rows, rows, P(seq + dp, None)), check_vma=False)
```

```python
import jax
import jax.numpy as jnp
from jax import lax
from jax.sharding import Mesh, PartitionSpec as P
from jax.experimental import pallas as pl
from jax.experimental.pallas import tpu as pltpu

bf = jnp.bfloat16
f32 = jnp.float32
HEADS = 8
D = 128
ROWS = 128
LANES = HEADS * ROWS
HALF = LANES // 2
SCALE = D ** -0.5
LOG = SCALE * 1.4426950408889634
CHUNK = 512
BLOCKS = CHUNK // ROWS
XCOLS = 1280


def dot(a, b, ca, cb):
    return lax.dot_general(a, b, (((ca,), (cb,)), ((), ())), preferred_element_type=f32)


def cols(index, width):
    return pl.ds(pl.multiple_of(index * width, width), width)


def remote(src, dst, sems, at, peer, there=None):
    return pltpu.make_async_remote_copy(src_ref=src, dst_ref=dst, send_sem=sems[0].at[at],
                                        recv_sem=sems[1].at[at if there is None else there],
                                        device_id=peer, device_id_type=pl.DeviceIdType.MESH)


def arrived(ref, sem):
    pltpu.make_async_copy(ref, ref, sem).wait()


def kernel(q, g, o, k, v, xin, dqo, dko, dvo, wo,
           kv, kt, qr, gr, dr, xl, dl, qn, gn, rs, sh, S, E, dka, dva, dqt, partk, partv, rcvk, rcvv, fink, finv,
           xp, xr, xt, dvall, wrc, wrp, w3, wrh, *sems):
    (lg, lo), sk, sv, sq, sg, sd, sx, sb, sc, sc2, sdq, spk, spv, srk, srv, sdv, swc, swp, swh = [
        sems[i:i + 2] for i in range(0, 38, 2)]
    x, z, y, h, c = (lax.axis_index(a) for a in ("x", "z", "y", "h", "c"))
    me = 8 * x + 4 * z + y

    def mod4(i):
        return lax.rem(i + 4, 4)

    xs = [mod4(x + d) for d in range(4)]
    ys = [mod4(y + e) for e in range(4)]
    hs = [mod4(h + e) for e in range(4)]
    near = [(dz, e) for dz in range(2) for e in range(4) if dz or e]

    def in_plane(dz, e):
        return {"z": (1 - z) if dz else z, "y": ys[e]}

    def in_side(dz, d):
        return {"x": xs[d], "z": (1 - z) if dz else z}

    barrier = pltpu.get_barrier_semaphore()
    friends = [{"x": xs[d], "y": ys[e]} for d in range(4) for e in range(4) if d or e]
    friends += [in_plane(1, e) for e in range(4)] + [in_side(1, d) for d in (1, 2, 3)]
    friends += [{"c": 1 - c}] + [{"h": hs[e]} for e in (1, 2, 3)]
    for friend in friends:
        pl.semaphore_signal(barrier, inc=1, device_id=friend, device_id_type=pl.DeviceIdType.MESH)
    get_g = [pltpu.make_async_copy(g.at[0, :, cols(j, LANES)], xp.at[j, :, 0:LANES], lg.at[j]) for j in range(4)]
    get_o = pltpu.make_async_copy(o.at[0], xl.at[:, 0:4 * LANES], lo)
    get_x = pltpu.make_async_copy(xin.at[0], xl, lo)
    for copy in get_g:
        copy.start()
    get_o.start()
    pl.semaphore_wait(barrier, len(friends))

    sends = []

    def send(*a):
        copy = remote(*a)
        copy.start()
        sends.append(copy)

    def spread(src, dst, s, width, which):
        for d in which:
            send(src.at[0, :, cols(xs[d], width)], dst, s, d, {"x": xs[d]})

    def stay(src, dst, s, width):
        pltpu.make_async_copy(src.at[0, :, cols(x, width)], dst, s[1].at[0]).start()

    spread(k, kv.at[me, :, 0:D], sk, D, (1, 3, 2))
    spread(v, kv.at[me, :, D:2 * D], sv, D, (1, 3, 2))
    stay(k, kv.at[me, :, 0:D], sk, D)
    stay(v, kv.at[me, :, D:2 * D], sv, D)
    spread(q, qr.at[x], sq, LANES, (1, 3, 2))
    stay(q, qr.at[x], sq, LANES)
    stay(g, gr.at[x], sg, LANES)

    for copy in get_g:
        copy.wait()
    get_o.wait()
    head = lax.broadcasted_iota(jnp.int32, (HEADS, LANES), 0)
    ones = jnp.where(head == lax.broadcasted_iota(jnp.int32, (HEADS, LANES), 1) // D, 1.0, 0.0).astype(bf)
    for j in range(4):
        at = slice(j * LANES, (j + 1) * LANES)
        prod = xp[j, :, 0:LANES].astype(f32) * xl[:, at].astype(f32)
        high = prod.astype(bf)
        low = (prod - high.astype(f32)).astype(bf)
        dl[j] = dot(ones, high, 1, 1) + dot(ones, low, 1, 1)
    get_x.start()
    for d in (1, 3, 2):
        send(dl.at[xs[d]], dr.at[x], sd, d, {"x": xs[d]})
    pltpu.make_async_copy(dl.at[x], dr.at[x], sd[1].at[0]).start()

    def slot(s, zz, yy):
        return kv.at[8 * s + 4 * zz + yy]

    for s in range(4):
        d = mod4(x - s)
        mine = slot(s, z, y)
        arrived(mine.at[:, 0:D], sk[1].at[d])
        arrived(mine.at[:, D:2 * D], sv[1].at[d])
        send(mine, mine, sb, (s, 0), {"z": 1 - z})
        for e in (1, 3, 2):
            send(mine, mine, sc, (s, e), {"y": ys[e]})

    get_x.wait()
    for j in range(4):
        xp[j] = jnp.concatenate([xl[:, 640 * b + 160 * j:640 * b + 160 * j + 160] for b in range(8)], axis=1)
    dka[...] = jnp.zeros_like(dka)
    dqt[...] = jnp.zeros_like(dqt)

    for s in (0, 1):
        theirs = slot(s + 2, 1 - z, y)
        arrived(theirs, sb[1].at[s + 2, 0])
        for e in (1, 3, 2):
            send(theirs, theirs, sc2, (s + 2, e), {"y": ys[e]})
        for e in (1, 3, 2):
            theirs = slot(s, z, mod4(y - e))
            arrived(theirs, sc[1].at[s, e])
            send(theirs, theirs, sb, (s, e), {"z": 1 - z})
    spread(g, gr.at[x], sg, LANES, (1, 3, 2))
    for e in (1, 3, 2):
        remote(xp.at[ys[e]], xr.at[y], sx, e, {"y": ys[e]}).start()
    pltpu.make_async_copy(xp.at[y], xr.at[y], sx[1].at[0]).start()

    def chunk_of(ch):
        return pl.ds(ch * BLOCKS, BLOCKS)

    def stats(s, carry):
        d = mod4(x - s)
        i = 8 * s + 4 * z + y

        @pl.when(s < 2)
        def _():
            for e in range(4):
                arrived(slot(s, 1 - z, mod4(y - e)), sb[1].at[s, e])

        @pl.when(s >= 2)
        def _():
            for e in (1, 2, 3):
                arrived(slot(s, z, mod4(y - e)), sc[1].at[s, e])
                arrived(slot(s, 1 - z, mod4(y - e)), sc2[1].at[s, e])

        for b in range(8):
            kt[:, cols(8 * s + b, D)] = kv[8 * s + b, :, 0:D].T
        arrived(qr.at[s], sq[1].at[d])
        arrived(dr.at[s], sd[1].at[d])
        for n in range(HEADS):
            cs = slice(n * D, (n + 1) * D)
            qn[s, cs, :] = qr[s, :, cs]
        n = 2 * s + z

        def half(side, carry):
            lanes = cols(side, HALF)

            def rows_of(ch, count, first=0):
                return pl.ds(pl.multiple_of((first + ch) * CHUNK, CHUNK), count * CHUNK)

            def score(ch, count):
                keys = kv[pl.ds(ch * BLOCKS, count * BLOCKS), :, 0:D].reshape(count * CHUNK, D)
                return dot(keys, qn[s, lanes, :], 1, 1)

            def top(m, t):
                return jnp.maximum(m, jnp.max(t.reshape(-1, 8, HALF), axis=0))

            def p1(ch, m, count):
                t = score(ch, count)
                S[rows_of(ch, count), :] = t
                return top(m, t)

            m = lax.fori_loop(0, s, lambda p, m: p1(2 * p, m, 2), jnp.full((8, HALF), -1e30, f32))
            m = lax.fori_loop(2 * s, n, lambda ch, m: p1(ch, m, 1), m)
            last = score(n, 1)
            key = n * CHUNK + lax.broadcasted_iota(jnp.int32, (CHUNK, 1), 0)
            row = i * ROWS + lax.broadcasted_iota(jnp.int32, (1, HALF), 1) % ROWS
            last = jnp.where(key <= row, last, -1e30)
            S[rows_of(n, 1), :] = last
            mc = jnp.max(top(m, last), axis=0, keepdims=True) * LOG

            def p2(ch, total, count):
                e = jnp.exp2(S[rows_of(ch, count), :] * LOG - mc)
                E[rows_of(ch, count, s * (s + 1)), lanes] = e.astype(bf)
                return total + jnp.sum(e.reshape(-1, 8, HALF), axis=0)

            total = lax.fori_loop(0, s, lambda p, t: p2(2 * p, t, 2), jnp.zeros((8, HALF), f32))
            total = lax.fori_loop(2 * s, n + 1, lambda ch, t: p2(ch, t, 1), total)
            rs[s, :, lanes] = 1.0 / jnp.sum(total, axis=0, keepdims=True)
            return carry

        lax.fori_loop(0, 2, half, 0)
        sh[s] = jnp.concatenate([dr[s, a:a + 1, :] for a in range(HEADS)], axis=1) * rs[s]
        return carry

    def scale(s, carry):
        arrived(gr.at[s], sg[1].at[mod4(x - s)])
        heads = jnp.concatenate([rs[s, :, n * D:(n + 1) * D] for n in range(HEADS)], axis=0).T
        for n in range(HEADS):
            cs = slice(n * D, (n + 1) * D)
            gn[s, cs, :] = (gr[s, :, cs].astype(f32) * heads[:, n:n + 1]).astype(bf)
        return carry

    def grads(s, ch, e32):
        at = cols(ch, CHUNK)
        values = kv[chunk_of(ch), :, D:2 * D].reshape(CHUNK, D)
        ds = (e32 * (dot(values, gn[s], 1, 1) - sh[s])).astype(bf)
        dka[at, :] += dot(ds, qn[s], 1, 0)
        dqt[s] += dot(kt[:, at], ds, 1, 0)

    def narrow(s, first, end):
        def one(ch, carry):
            grads(s, ch, E[cols(s * (s + 1) + ch, CHUNK), :].astype(f32))
            return carry

        lax.fori_loop(first, end, one, 0)

    def give_dq(s):
        for n in range(HEADS):
            cs = slice(n * D, (n + 1) * D)
            xl[:, cols(s * HEADS + n, D)] = (dqt[s, :, cs] * SCALE).astype(bf).T
        home = dqo.at[0, :, cols(x, LANES)]

        @pl.when(s == x)
        def _():
            pltpu.make_async_copy(xl.at[:, cols(s, LANES)], home, sdq[1].at[0]).start()

        @pl.when(s != x)
        def _():
            remote(xl.at[:, cols(s, LANES)], home, sdq, mod4(s - x), {"x": s}).start()

    def total_of(part, rcv, sems, s):
        def add(n, total):
            arrived(rcv.at[n, s], sems[1].at[n, s])
            return total + rcv[n, s].astype(f32)

        return lax.fori_loop(1, 8, add, part[s, 4 * z + y].astype(f32)).astype(bf)

    def deliver(src, dst, s2, at, there, s):
        @pl.when(s == x)
        def _():
            pltpu.make_async_copy(src, dst, s2[1].at[there]).start()

        @pl.when(s != x)
        def _():
            remote(src, dst, s2, at, {"x": s}, there).start()

    def reduce_v(s):
        finv[s] = total_of(partv, rcvv, spv, s)
        place = dvall.at[y, :, cols(x, D)]
        for e in (1, 3, 2):
            remote(finv.at[s], place, sdv, (s, e), {"x": s, "y": ys[e]}, (x, y)).start()
        deliver(finv.at[s], place, sdv, (s, 0), (x, y), s)
        deliver(finv.at[s], dvo.at[0, :, cols(x, D)], srv, s, x, s)

    def reduce_k(s):
        fink[s] = total_of(partk, rcvk, spk, s)
        deliver(fink.at[s], dko.at[0, :, cols(x, D)], srk, s, x, s)

    def hand_out(part, rcv, sems, a):
        def one(n, carry):
            to = {"z": lax.rem(z + n // 4, 2), "y": lax.rem(y + n, 4)}
            remote(part.at[a, 4 * to["z"] + to["y"]], rcv.at[n, a], sems, (n, a), to).start()
            return carry

        lax.fori_loop(1, 8, one, 0)

    def values_of(t, carry):
        a = 3 - t

        def share(s, ch, count):
            e = E[pl.ds(pl.multiple_of((s * (s + 1) + ch) * CHUNK, CHUNK), count * CHUNK), :]
            return dot(e, gn[s], 1, 0)

        dva[...] = jnp.zeros_like(dva)

        def both(s, carry):
            dva[...] += share(s, 2 * a, 2)
            return carry

        def one(zz, carry):
            dva[cols(zz, CHUNK), :] += share(a, 2 * a + zz, 1)
            return carry

        lax.fori_loop(a + 1, 4, both, 0)
        lax.fori_loop(0, 1 + z, one, 0)
        for b in range(8):
            partv[a, b] = dva[b * ROWS:(b + 1) * ROWS, :].astype(bf)
        hand_out(partv, rcvv, spv, a)
        return carry

    order = [(1, 2), (1, 1), (1, 3), (0, 2), (0, 1), (0, 3), (1, 0), (0, 0)]

    def piece(dz, d):
        peer = in_side(dz, d)
        return peer, 2 * peer["x"] + peer["z"]

    def turn_x():
        line = lax.broadcasted_iota(jnp.int32, (320, 640), 0)
        want = line + 20 * lax.shift_right_logical(line * 3277, 16)
        place = lax.broadcasted_iota(jnp.int32, (320, 640), 1)
        for e in range(4):
            arrived(xr.at[mod4(y - e)], sx[1].at[e])
        def turn(n, carry):
            part_c, half, j = n // 8, n // 4 % 2, n % 4
            pick = jnp.where(place == want + 20 * part_c, 1.0, 0.0).astype(bf)
            rows = dot(pick, xr[j, :, cols(half, 640)], 1, 1).astype(bf)
            xt[part_c, pl.ds(half * 4, 4), :, cols(j, ROWS)] = rows.reshape(4, 80, ROWS)
            return carry

        lax.fori_loop(0, 16, turn, 0)

    def weigh():
        def wait(n, carry):
            arrived(dvall.at[n % 4, :, cols(n // 4, D)], sdv[1].at[n // 4, n % 4])
            return carry

        lax.fori_loop(0, 16, wait, 0)
        tall = dvall[...].reshape(4 * ROWS, 4 * D)

        def product(half, carry):
            xt[half] = dot(xt[half].reshape(640, 4 * ROWS), tall, 1, 0).astype(bf).reshape(8, 80, 4 * D)
            return carry

        lax.fori_loop(0, 2, product, 0)
        for n, (dz, d) in enumerate(order):
            b = piece(dz, d)[1]
            remote(xt.at[1 - c, b], wrc.at[b], swc, n, {"c": 1 - c}).start()

    def over_sides():
        for n, (dz, d) in enumerate(order):
            peer, b = piece(dz, d)
            arrived(wrc.at[b], swc[1].at[n])
            wrc[b] = (xt[c, b].astype(f32) + wrc[b].astype(f32)).astype(bf)
            if dz or d:
                remote(wrc.at[b], wrp.at[dz * 4 + d], swp, dz * 4 + d, peer).start()

    def over_rest():
        total = wrc[2 * x + z].astype(f32)
        for dz, d in near:
            n = dz * 4 + d
            arrived(wrp.at[n], swp[1].at[n])
            total = total + wrp[n].astype(f32)
        for e in range(4):
            w3[e] = jnp.concatenate([total[20 * e:20 * e + 20], jnp.zeros((12, 4 * D), f32)], axis=0).astype(bf)
        for e in (1, 3, 2):
            remote(w3.at[hs[e]], wrh.at[e], swh, e, {"h": hs[e]}).start()

    def give_two(first):
        lax.fori_loop(first, first + 2, lambda s, carry: (give_dq(s), carry)[1], 0)

    def step(t, carry):
        early = 1 - jnp.minimum(t // 2, 1)
        a = (1 - early) * (3 - (t - 2) // 2)
        s = early * t + (1 - early) * (3 - t % 2)
        narrow(s, 2 * a, jnp.minimum(2 * a + 2 + 2 * early, 2 * s + 1 + z))

        @pl.when(t == 0)
        def _():
            turn_x()
            lax.fori_loop(0, 4, lambda n, carry: (reduce_v(3 - n), carry)[1], 0)

        @pl.when(jnp.logical_and(t > 1, t % 2 == 1))
        def _():
            def one(b, carry):
                partk[a, b] = (dka[cols(8 * a + b, ROWS), :] * SCALE).astype(bf)
                return carry

            lax.fori_loop(0, 8, one, 0)
            hand_out(partk, rcvk, spk, a)

        @pl.when(jnp.logical_and(t > 4, t % 2 == 1))
        def _():
            reduce_k(a + 1)


        pl.when(t == 1)(weigh)
        pl.when(t == 3)(over_sides)
        pl.when(t == 3)(lambda: give_two(0))
        pl.when(t == 7)(over_rest)
        return carry

    lax.fori_loop(0, 4, stats, 0)
    lax.fori_loop(0, 4, scale, 0)
    lax.fori_loop(0, 4, values_of, 0)
    lax.fori_loop(0, 10, step, 0)
    give_two(2)
    last = w3[h].astype(f32)
    for e in (1, 3, 2):
        arrived(wrh.at[e], swh[1].at[e])
        last = last + wrh[e].astype(f32)
    wo[...] = last[0:20]
    reduce_k(0)

    for d in range(4):
        f = mod4(x - d)
        arrived(dqo.at[0, :, cols(f, LANES)], sdq[1].at[d])
        arrived(dko.at[0, :, cols(d, D)], srk[1].at[d])
        arrived(dvo.at[0, :, cols(d, D)], srv[1].at[d])
    for copy in sends:
        copy.wait_send()
    for e in (1, 2, 3):
        remote(xp.at[ys[e]], xr.at[y], sx, e, {"y": ys[e]}).wait_send()
    for d in (1, 2, 3):
        remote(xl.at[:, cols(xs[d], LANES)], dqo.at[0, :, cols(x, LANES)], sdq, d, {"x": xs[d]}).wait_send()
    def sent(n, carry):
        to = {"z": lax.rem(z + n // 4, 2), "y": lax.rem(y + n, 4)}
        for a in range(4):
            remote(partk.at[a, 0], rcvk.at[n, a], spk, (n, a), to).wait_send()
            remote(partv.at[a, 0], rcvv.at[n, a], spv, (n, a), to).wait_send()
        return carry

    lax.fori_loop(1, 8, sent, 0)
    for s in range(4):
        for e in (1, 2, 3):
            remote(finv.at[s], dvall.at[y, :, cols(x, D)], sdv, (s, e), {"y": ys[e]}).wait_send()
    for d in (1, 2, 3):
        t = xs[d]
        remote(finv.at[t], dvall.at[y, :, cols(x, D)], sdv, (t, 0), {"x": t}).wait_send()
        remote(fink.at[t], dko.at[0, :, cols(x, D)], srk, t, {"x": t}).wait_send()
        remote(finv.at[t], dvo.at[0, :, cols(x, D)], srv, t, {"x": t}).wait_send()
    for n, (dz, d) in enumerate(order):
        peer, b = piece(dz, d)
        remote(xt.at[1 - c, b], wrc.at[b], swc, n, {"c": 1 - c}).wait_send()
        if dz or d:
            remote(wrc.at[b], wrp.at[dz * 4 + d], swp, dz * 4 + d, peer).wait_send()
    for e in (1, 2, 3):
        remote(w3.at[hs[e]], wrh.at[e], swh, e, {"h": hs[e]}).wait_send()


def per_device(x_in, q, k, v, o, g):
    T = 32 * ROWS
    anyspace = pl.BlockSpec(memory_space=pl.ANY)
    sems = [(4,), ()] + [(4,)] * 12 + [(4, 4)] * 6 + [(4,)] * 2 + [(8, 4)] * 4 + [(4,)] * 4 + [(4, 4)] * 2 + [(8,)] * 2
    sems += [(8,)] * 2 + [(4,)] * 2
    tall = (T, D)
    scratch = [((32, ROWS, 2 * D), bf), ((D, T), bf), ((4, ROWS, LANES), bf), ((4, ROWS, LANES), bf), ((4, HEADS, ROWS), f32),
               ((ROWS, 4 * XCOLS), bf), ((4, HEADS, ROWS), f32),
               ((4, LANES, D), bf), ((4, LANES, D), bf), ((4, 1, LANES), f32), ((4, 1, LANES), f32),
               ((T, HALF), f32), ((20 * CHUNK, LANES), bf), (tall, f32), ((2 * CHUNK, D), f32), ((4, D, LANES), f32),
               ((4, 8, ROWS, D), bf), ((4, 8, ROWS, D), bf), ((8, 4, ROWS, D), bf),
               ((8, 4, ROWS, D), bf), ((4, ROWS, D), bf), ((4, ROWS, D), bf),
               ((4, ROWS, XCOLS), bf), ((4, ROWS, XCOLS), bf), ((2, 8, 80, 4 * ROWS), bf), ((4, ROWS, 4 * D), bf),
               ((8, 80, 4 * D), bf), ((8, 80, 4 * D), bf),
               ((4, 32, 4 * D), bf), ((4, 32, 4 * D), bf)]
    return pl.pallas_call(
        kernel,
        out_shape=[jax.ShapeDtypeStruct((1, ROWS, 4 * LANES), bf), jax.ShapeDtypeStruct((1, ROWS, 4 * D), bf),
                   jax.ShapeDtypeStruct((1, ROWS, 4 * D), bf), jax.ShapeDtypeStruct((20, 4 * D), f32)],
        in_specs=[anyspace] * 6,
        out_specs=[anyspace] * 3 + [pl.BlockSpec(memory_space=pltpu.VMEM)],
        scratch_shapes=[pltpu.VMEM(*s) for s in scratch] + [pltpu.SemaphoreType.DMA(s) for s in sems],
        compiler_params=pltpu.CompilerParams(vmem_limit_bytes=60 << 20, collective_id=0, has_side_effects=True),
        name="attention_backward")(q, g, o, k, v, x_in)


def solution(mesh):
    fine = Mesh(mesh.devices.reshape(4, 2, 4, 4, 2), ("x", "z", "y", "h", "c"))
    seq, dp = ("x", "z", "y"), ("h", "c")
    rows = P(dp, seq, None)
    return jax.shard_map(per_device, mesh=fine, in_specs=(rows,) * 6,
                         out_specs=(rows, rows, rows, P(seq + dp, None)), check_vma=False)
```

```python
import jax
import jax.numpy as jnp
from jax import lax
from jax.sharding import Mesh, PartitionSpec as P
from jax.experimental import pallas as pl
from jax.experimental.pallas import tpu as pltpu

bf = jnp.bfloat16
f32 = jnp.float32
HEADS = 8
D = 128
ROWS = 128
LANES = HEADS * ROWS
HALF = LANES // 2
SCALE = D ** -0.5
LOG = SCALE * 1.4426950408889634
CHUNK = 512
BLOCKS = CHUNK // ROWS
XCOLS = 1280


def dot(a, b, ca, cb):
    return lax.dot_general(a, b, (((ca,), (cb,)), ((), ())), preferred_element_type=f32)


def cols(index, width):
    return pl.ds(pl.multiple_of(index * width, width), width)


def remote(src, dst, sems, at, peer, there=None):
    return pltpu.make_async_remote_copy(src_ref=src, dst_ref=dst, send_sem=sems[0].at[at],
                                        recv_sem=sems[1].at[at if there is None else there],
                                        device_id=peer, device_id_type=pl.DeviceIdType.MESH)


def arrived(ref, sem):
    pltpu.make_async_copy(ref, ref, sem).wait()


def kernel(q, g, o, k, v, xin, dqo, dko, dvo, wo,
           kv, kt, qr, gr, dr, xl, dl, qn, gn, rs, sh, S, E, dka, dva, dqt, partk, partv, rcvk, rcvv, fink, finv,
           xp, xr, xt, dvall, wrc, wrp, w3, wrh, *sems):
    (lg, lo), sk, sv, sq, sg, sd, sx, sb, sc, sc2, sdq, spk, spv, srk, srv, sdv, swc, swp, swh = [
        sems[i:i + 2] for i in range(0, 38, 2)]
    x, z, y, h, c = (lax.axis_index(a) for a in ("x", "z", "y", "h", "c"))
    me = 8 * x + 4 * z + y

    def mod4(i):
        return lax.rem(i + 4, 4)

    xs = [mod4(x + d) for d in range(4)]
    ys = [mod4(y + e) for e in range(4)]
    hs = [mod4(h + e) for e in range(4)]
    near = [(dz, e) for dz in range(2) for e in range(4) if dz or e]

    def in_plane(dz, e):
        return {"z": (1 - z) if dz else z, "y": ys[e]}

    def in_side(dz, d):
        return {"x": xs[d], "z": (1 - z) if dz else z}

    barrier = pltpu.get_barrier_semaphore()
    friends = [{"x": xs[d], "y": ys[e]} for d in range(4) for e in range(4) if d or e]
    friends += [in_plane(1, e) for e in range(4)] + [in_side(1, d) for d in (1, 2, 3)]
    friends += [{"c": 1 - c}] + [{"h": hs[e]} for e in (1, 2, 3)]
    for friend in friends:
        pl.semaphore_signal(barrier, inc=1, device_id=friend, device_id_type=pl.DeviceIdType.MESH)
    get_g = [pltpu.make_async_copy(g.at[0, :, cols(j, LANES)], xp.at[j, :, 0:LANES], lg.at[j]) for j in range(4)]
    get_o = pltpu.make_async_copy(o.at[0], xl.at[:, 0:4 * LANES], lo)
    get_x = pltpu.make_async_copy(xin.at[0], xl, lo)
    for copy in get_g:
        copy.start()
    get_o.start()
    pl.semaphore_wait(barrier, len(friends))

    sends = []

    def send(*a):
        copy = remote(*a)
        copy.start()
        sends.append(copy)

    def spread(src, dst, s, width, which):
        for d in which:
            send(src.at[0, :, cols(xs[d], width)], dst, s, d, {"x": xs[d]})

    def stay(src, dst, s, width):
        pltpu.make_async_copy(src.at[0, :, cols(x, width)], dst, s[1].at[0]).start()

    spread(k, kv.at[me, :, 0:D], sk, D, (1, 3, 2))
    spread(v, kv.at[me, :, D:2 * D], sv, D, (1, 3, 2))
    stay(k, kv.at[me, :, 0:D], sk, D)
    stay(v, kv.at[me, :, D:2 * D], sv, D)
    spread(q, qr.at[x], sq, LANES, (1, 3, 2))
    stay(q, qr.at[x], sq, LANES)
    stay(g, gr.at[x], sg, LANES)

    for copy in get_g:
        copy.wait()
    get_o.wait()
    head = lax.broadcasted_iota(jnp.int32, (HEADS, LANES), 0)
    ones = jnp.where(head == lax.broadcasted_iota(jnp.int32, (HEADS, LANES), 1) // D, 1.0, 0.0).astype(bf)
    for j in range(4):
        at = slice(j * LANES, (j + 1) * LANES)
        prod = xp[j, :, 0:LANES].astype(f32) * xl[:, at].astype(f32)
        high = prod.astype(bf)
        low = (prod - high.astype(f32)).astype(bf)
        dl[j] = dot(ones, high, 1, 1) + dot(ones, low, 1, 1)
    get_x.start()
    for d in (1, 3, 2):
        send(dl.at[xs[d]], dr.at[x], sd, d, {"x": xs[d]})
    pltpu.make_async_copy(dl.at[x], dr.at[x], sd[1].at[0]).start()

    def slot(s, zz, yy):
        return kv.at[8 * s + 4 * zz + yy]

    for s in range(4):
        d = mod4(x - s)
        mine = slot(s, z, y)
        arrived(mine.at[:, 0:D], sk[1].at[d])
        arrived(mine.at[:, D:2 * D], sv[1].at[d])
        send(mine, mine, sb, (s, 0), {"z": 1 - z})
        for e in (1, 3, 2):
            send(mine, mine, sc, (s, e), {"y": ys[e]})

    get_x.wait()
    for j in range(4):
        xp[j] = jnp.concatenate([xl[:, 640 * b + 160 * j:640 * b + 160 * j + 160] for b in range(8)], axis=1)
    dka[...] = jnp.zeros_like(dka)
    dqt[...] = jnp.zeros_like(dqt)

    for s in (0, 1):
        theirs = slot(s + 2, 1 - z, y)
        arrived(theirs, sb[1].at[s + 2, 0])
        for e in (1, 3, 2):
            send(theirs, theirs, sc2, (s + 2, e), {"y": ys[e]})
        for e in (1, 3, 2):
            theirs = slot(s, z, mod4(y - e))
            arrived(theirs, sc[1].at[s, e])
            send(theirs, theirs, sb, (s, e), {"z": 1 - z})
    spread(g, gr.at[x], sg, LANES, (1, 3, 2))
    for e in (1, 3, 2):
        remote(xp.at[ys[e]], xr.at[y], sx, e, {"y": ys[e]}).start()
    pltpu.make_async_copy(xp.at[y], xr.at[y], sx[1].at[0]).start()

    def chunk_of(ch):
        return pl.ds(ch * BLOCKS, BLOCKS)

    def stats(s, carry):
        d = mod4(x - s)
        i = 8 * s + 4 * z + y

        @pl.when(s < 2)
        def _():
            for e in range(4):
                arrived(slot(s, 1 - z, mod4(y - e)), sb[1].at[s, e])

        @pl.when(s >= 2)
        def _():
            for e in (1, 2, 3):
                arrived(slot(s, z, mod4(y - e)), sc[1].at[s, e])
                arrived(slot(s, 1 - z, mod4(y - e)), sc2[1].at[s, e])

        for b in range(8):
            kt[:, cols(8 * s + b, D)] = kv[8 * s + b, :, 0:D].T
        arrived(qr.at[s], sq[1].at[d])
        arrived(dr.at[s], sd[1].at[d])
        for n in range(HEADS):
            cs = slice(n * D, (n + 1) * D)
            qn[s, cs, :] = qr[s, :, cs]
        n = 2 * s + z

        def half(side, carry):
            lanes = cols(side, HALF)

            def rows_of(ch, count, first=0):
                return pl.ds(pl.multiple_of((first + ch) * CHUNK, CHUNK), count * CHUNK)

            def score(ch, count):
                keys = kv[pl.ds(ch * BLOCKS, count * BLOCKS), :, 0:D].reshape(count * CHUNK, D)
                return dot(keys, qn[s, lanes, :], 1, 1)

            def top(m, t):
                return jnp.maximum(m, jnp.max(t.reshape(-1, 8, HALF), axis=0))

            def p1(ch, m, count):
                t = score(ch, count)
                S[rows_of(ch, count), :] = t
                return top(m, t)

            m = lax.fori_loop(0, s, lambda p, m: p1(2 * p, m, 2), jnp.full((8, HALF), -1e30, f32))
            m = lax.fori_loop(2 * s, n, lambda ch, m: p1(ch, m, 1), m)
            last = score(n, 1)
            key = n * CHUNK + lax.broadcasted_iota(jnp.int32, (CHUNK, 1), 0)
            row = i * ROWS + lax.broadcasted_iota(jnp.int32, (1, HALF), 1) % ROWS
            last = jnp.where(key <= row, last, -1e30)
            S[rows_of(n, 1), :] = last
            mc = jnp.max(top(m, last), axis=0, keepdims=True) * LOG

            def p2(ch, total, count):
                e = jnp.exp2(S[rows_of(ch, count), :] * LOG - mc)
                E[rows_of(ch, count, s * (s + 1)), lanes] = e.astype(bf)
                return total + jnp.sum(e.reshape(-1, 8, HALF), axis=0)

            total = lax.fori_loop(0, s, lambda p, t: p2(2 * p, t, 2), jnp.zeros((8, HALF), f32))
            total = lax.fori_loop(2 * s, n + 1, lambda ch, t: p2(ch, t, 1), total)
            rs[s, :, lanes] = 1.0 / jnp.sum(total, axis=0, keepdims=True)
            return carry

        lax.fori_loop(0, 2, half, 0)
        sh[s] = jnp.concatenate([dr[s, a:a + 1, :] for a in range(HEADS)], axis=1) * rs[s]
        return carry

    def scale(s, carry):
        arrived(gr.at[s], sg[1].at[mod4(x - s)])
        heads = jnp.concatenate([rs[s, :, n * D:(n + 1) * D] for n in range(HEADS)], axis=0).T
        for n in range(HEADS):
            cs = slice(n * D, (n + 1) * D)
            gn[s, cs, :] = (gr[s, :, cs].astype(f32) * heads[:, n:n + 1]).astype(bf)
        return carry

    def grads(s, ch, e32):
        at = cols(ch, CHUNK)
        values = kv[chunk_of(ch), :, D:2 * D].reshape(CHUNK, D)
        ds = (e32 * (dot(values, gn[s], 1, 1) - sh[s])).astype(bf)
        dka[at, :] += dot(ds, qn[s], 1, 0)
        dqt[s] += dot(kt[:, at], ds, 1, 0)

    def narrow(s, first, end):
        def one(ch, carry):
            grads(s, ch, E[cols(s * (s + 1) + ch, CHUNK), :].astype(f32))
            return carry

        lax.fori_loop(first, end, one, 0)

    def give_dq(s):
        for n in range(HEADS):
            cs = slice(n * D, (n + 1) * D)
            xl[:, cols(s * HEADS + n, D)] = (dqt[s, :, cs] * SCALE).astype(bf).T
        home = dqo.at[0, :, cols(x, LANES)]

        @pl.when(s == x)
        def _():
            pltpu.make_async_copy(xl.at[:, cols(s, LANES)], home, sdq[1].at[0]).start()

        @pl.when(s != x)
        def _():
            remote(xl.at[:, cols(s, LANES)], home, sdq, mod4(s - x), {"x": s}).start()

    def total_of(part, rcv, sems, s):
        def add(n, total):
            arrived(rcv.at[n, s], sems[1].at[n, s])
            return total + rcv[n, s].astype(f32)

        return lax.fori_loop(1, 8, add, part[s, 4 * z + y].astype(f32)).astype(bf)

    def deliver(src, dst, s2, at, there, s):
        @pl.when(s == x)
        def _():
            pltpu.make_async_copy(src, dst, s2[1].at[there]).start()

        @pl.when(s != x)
        def _():
            remote(src, dst, s2, at, {"x": s}, there).start()

    def reduce_v(s):
        finv[s] = total_of(partv, rcvv, spv, s)
        place = dvall.at[y, :, cols(x, D)]
        for e in (1, 3, 2):
            remote(finv.at[s], place, sdv, (s, e), {"x": s, "y": ys[e]}, (x, y)).start()
        deliver(finv.at[s], place, sdv, (s, 0), (x, y), s)
        deliver(finv.at[s], dvo.at[0, :, cols(x, D)], srv, s, x, s)

    def reduce_k(s):
        fink[s] = total_of(partk, rcvk, spk, s)
        deliver(fink.at[s], dko.at[0, :, cols(x, D)], srk, s, x, s)

    def hand_out(part, rcv, sems, a):
        def one(n, carry):
            to = {"z": lax.rem(z + n // 4, 2), "y": lax.rem(y + n, 4)}
            remote(part.at[a, 4 * to["z"] + to["y"]], rcv.at[n, a], sems, (n, a), to).start()
            return carry

        lax.fori_loop(1, 8, one, 0)

    def values_of(t, carry):
        a = 3 - t

        def share(s, ch, count):
            e = E[pl.ds(pl.multiple_of((s * (s + 1) + ch) * CHUNK, CHUNK), count * CHUNK), :]
            return dot(e, gn[s], 1, 0)

        dva[...] = jnp.zeros_like(dva)

        def both(s, carry):
            dva[...] += share(s, 2 * a, 2)
            return carry

        def one(zz, carry):
            dva[cols(zz, CHUNK), :] += share(a, 2 * a + zz, 1)
            return carry

        lax.fori_loop(a + 1, 4, both, 0)
        lax.fori_loop(0, 1 + z, one, 0)
        for b in range(8):
            partv[a, b] = dva[b * ROWS:(b + 1) * ROWS, :].astype(bf)
        hand_out(partv, rcvv, spv, a)
        return carry

    order = [(1, 2), (1, 1), (1, 3), (0, 2), (0, 1), (0, 3), (1, 0), (0, 0)]

    def piece(dz, d):
        peer = in_side(dz, d)
        return peer, 2 * peer["x"] + peer["z"]

    def turn_x():
        line = lax.broadcasted_iota(jnp.int32, (320, 640), 0)
        want = line + 20 * lax.shift_right_logical(line * 3277, 16)
        place = lax.broadcasted_iota(jnp.int32, (320, 640), 1)
        for e in range(4):
            arrived(xr.at[mod4(y - e)], sx[1].at[e])
        def turn(n, carry):
            part_c, half, j = n // 8, n // 4 % 2, n % 4
            pick = jnp.where(place == want + 20 * part_c, 1.0, 0.0).astype(bf)
            rows = dot(pick, xr[j, :, cols(half, 640)], 1, 1).astype(bf)
            xt[part_c, pl.ds(half * 4, 4), :, cols(j, ROWS)] = rows.reshape(4, 80, ROWS)
            return carry

        lax.fori_loop(0, 16, turn, 0)

    def weigh():
        def wait(n, carry):
            arrived(dvall.at[n % 4, :, cols(n // 4, D)], sdv[1].at[n // 4, n % 4])
            return carry

        lax.fori_loop(0, 16, wait, 0)
        tall = dvall[...].reshape(4 * ROWS, 4 * D)

        def product(half, carry):
            xt[half] = dot(xt[half].reshape(640, 4 * ROWS), tall, 1, 0).astype(bf).reshape(8, 80, 4 * D)
            return carry

        lax.fori_loop(0, 2, product, 0)
        for n, (dz, d) in enumerate(order):
            b = piece(dz, d)[1]
            remote(xt.at[1 - c, b], wrc.at[b], swc, n, {"c": 1 - c}).start()

    def over_sides():
        for n, (dz, d) in enumerate(order):
            peer, b = piece(dz, d)
            arrived(wrc.at[b], swc[1].at[n])
            wrc[b] = (xt[c, b].astype(f32) + wrc[b].astype(f32)).astype(bf)
            if dz or d:
                remote(wrc.at[b], wrp.at[dz * 4 + d], swp, dz * 4 + d, peer).start()

    def over_rest():
        total = wrc[2 * x + z].astype(f32)
        for dz, d in near:
            n = dz * 4 + d
            arrived(wrp.at[n], swp[1].at[n])
            total = total + wrp[n].astype(f32)
        for e in range(4):
            w3[e] = jnp.concatenate([total[20 * e:20 * e + 20], jnp.zeros((12, 4 * D), f32)], axis=0).astype(bf)
        for e in (1, 3, 2):
            remote(w3.at[hs[e]], wrh.at[e], swh, e, {"h": hs[e]}).start()

    def give_two(first):
        lax.fori_loop(first, first + 2, lambda s, carry: (give_dq(s), carry)[1], 0)

    def step(t, carry):
        early = 1 - jnp.minimum(t // 2, 1)
        a = (1 - early) * (3 - (t - 2) // 2)
        s = early * t + (1 - early) * (3 - t % 2)
        narrow(s, 2 * a, jnp.minimum(2 * a + 2 + 2 * early, 2 * s + 1 + z))

        @pl.when(t == 0)
        def _():
            lax.fori_loop(0, 4, lambda n, carry: (reduce_v(3 - n), carry)[1], 0)

        @pl.when(jnp.logical_and(t > 1, t % 2 == 1))
        def _():
            def one(b, carry):
                partk[a, b] = (dka[cols(8 * a + b, ROWS), :] * SCALE).astype(bf)
                return carry

            lax.fori_loop(0, 8, one, 0)
            hand_out(partk, rcvk, spk, a)

        @pl.when(jnp.logical_and(t > 4, t % 2 == 1))
        def _():
            reduce_k(a + 1)


        pl.when(t == 1)(weigh)
        pl.when(t == 3)(over_sides)
        pl.when(t == 3)(lambda: give_two(0))
        pl.when(t == 8)(over_rest)
        return carry

    lax.fori_loop(0, 4, stats, 0)
    lax.fori_loop(0, 4, scale, 0)
    lax.fori_loop(0, 4, values_of, 0)
    turn_x()
    lax.fori_loop(0, 10, step, 0)
    give_two(2)
    reduce_k(0)
    last = w3[h].astype(f32)
    for e in (1, 3, 2):
        arrived(wrh.at[e], swh[1].at[e])
        last = last + wrh[e].astype(f32)
    wo[...] = last[0:20]

    for d in range(4):
        f = mod4(x - d)
        arrived(dqo.at[0, :, cols(f, LANES)], sdq[1].at[d])
        arrived(dko.at[0, :, cols(d, D)], srk[1].at[d])
        arrived(dvo.at[0, :, cols(d, D)], srv[1].at[d])
    for copy in sends:
        copy.wait_send()
    for e in (1, 2, 3):
        remote(xp.at[ys[e]], xr.at[y], sx, e, {"y": ys[e]}).wait_send()
    for d in (1, 2, 3):
        remote(xl.at[:, cols(xs[d], LANES)], dqo.at[0, :, cols(x, LANES)], sdq, d, {"x": xs[d]}).wait_send()
    def sent(n, carry):
        to = {"z": lax.rem(z + n // 4, 2), "y": lax.rem(y + n, 4)}
        for a in range(4):
            remote(partk.at[a, 0], rcvk.at[n, a], spk, (n, a), to).wait_send()
            remote(partv.at[a, 0], rcvv.at[n, a], spv, (n, a), to).wait_send()
        return carry

    lax.fori_loop(1, 8, sent, 0)
    for s in range(4):
        for e in (1, 2, 3):
            remote(finv.at[s], dvall.at[y, :, cols(x, D)], sdv, (s, e), {"y": ys[e]}).wait_send()
    for d in (1, 2, 3):
        t = xs[d]
        remote(finv.at[t], dvall.at[y, :, cols(x, D)], sdv, (t, 0), {"x": t}).wait_send()
        remote(fink.at[t], dko.at[0, :, cols(x, D)], srk, t, {"x": t}).wait_send()
        remote(finv.at[t], dvo.at[0, :, cols(x, D)], srv, t, {"x": t}).wait_send()
    for n, (dz, d) in enumerate(order):
        peer, b = piece(dz, d)
        remote(xt.at[1 - c, b], wrc.at[b], swc, n, {"c": 1 - c}).wait_send()
        if dz or d:
            remote(wrc.at[b], wrp.at[dz * 4 + d], swp, dz * 4 + d, peer).wait_send()
    for e in (1, 2, 3):
        remote(w3.at[hs[e]], wrh.at[e], swh, e, {"h": hs[e]}).wait_send()


def per_device(x_in, q, k, v, o, g):
    T = 32 * ROWS
    anyspace = pl.BlockSpec(memory_space=pl.ANY)
    sems = [(4,), ()] + [(4,)] * 12 + [(4, 4)] * 6 + [(4,)] * 2 + [(8, 4)] * 4 + [(4,)] * 4 + [(4, 4)] * 2 + [(8,)] * 2
    sems += [(8,)] * 2 + [(4,)] * 2
    tall = (T, D)
    scratch = [((32, ROWS, 2 * D), bf), ((D, T), bf), ((4, ROWS, LANES), bf), ((4, ROWS, LANES), bf), ((4, HEADS, ROWS), f32),
               ((ROWS, 4 * XCOLS), bf), ((4, HEADS, ROWS), f32),
               ((4, LANES, D), bf), ((4, LANES, D), bf), ((4, 1, LANES), f32), ((4, 1, LANES), f32),
               ((T, HALF), f32), ((20 * CHUNK, LANES), bf), (tall, f32), ((2 * CHUNK, D), f32), ((4, D, LANES), f32),
               ((4, 8, ROWS, D), bf), ((4, 8, ROWS, D), bf), ((8, 4, ROWS, D), bf),
               ((8, 4, ROWS, D), bf), ((4, ROWS, D), bf), ((4, ROWS, D), bf),
               ((4, ROWS, XCOLS), bf), ((4, ROWS, XCOLS), bf), ((2, 8, 80, 4 * ROWS), bf), ((4, ROWS, 4 * D), bf),
               ((8, 80, 4 * D), bf), ((8, 80, 4 * D), bf),
               ((4, 32, 4 * D), bf), ((4, 32, 4 * D), bf)]
    return pl.pallas_call(
        kernel,
        out_shape=[jax.ShapeDtypeStruct((1, ROWS, 4 * LANES), bf), jax.ShapeDtypeStruct((1, ROWS, 4 * D), bf),
                   jax.ShapeDtypeStruct((1, ROWS, 4 * D), bf), jax.ShapeDtypeStruct((20, 4 * D), f32)],
        in_specs=[anyspace] * 6,
        out_specs=[anyspace] * 3 + [pl.BlockSpec(memory_space=pltpu.VMEM)],
        scratch_shapes=[pltpu.VMEM(*s) for s in scratch] + [pltpu.SemaphoreType.DMA(s) for s in sems],
        compiler_params=pltpu.CompilerParams(vmem_limit_bytes=60 << 20, collective_id=0, has_side_effects=True),
        name="attention_backward")(q, g, o, k, v, x_in)


def solution(mesh):
    fine = Mesh(mesh.devices.reshape(4, 2, 4, 4, 2), ("x", "z", "y", "h", "c"))
    seq, dp = ("x", "z", "y"), ("h", "c")
    rows = P(dp, seq, None)
    return jax.shard_map(per_device, mesh=fine, in_specs=(rows,) * 6,
                         out_specs=(rows, rows, rows, P(seq + dp, None)), check_vma=False)
```

```python
import jax
import jax.numpy as jnp
from jax import lax
from jax.sharding import Mesh, PartitionSpec as P
from jax.experimental import pallas as pl
from jax.experimental.pallas import tpu as pltpu

bf = jnp.bfloat16
f32 = jnp.float32
HEADS = 8
D = 128
ROWS = 128
LANES = HEADS * ROWS
HALF = LANES // 2
SCALE = D ** -0.5
LOG = SCALE * 1.4426950408889634
CHUNK = 512
BLOCKS = CHUNK // ROWS
XCOLS = 1280


def dot(a, b, ca, cb):
    return lax.dot_general(a, b, (((ca,), (cb,)), ((), ())), preferred_element_type=f32)


def cols(index, width):
    return pl.ds(pl.multiple_of(index * width, width), width)


def remote(src, dst, sems, at, peer, there=None):
    return pltpu.make_async_remote_copy(src_ref=src, dst_ref=dst, send_sem=sems[0].at[at],
                                        recv_sem=sems[1].at[at if there is None else there],
                                        device_id=peer, device_id_type=pl.DeviceIdType.MESH)


def arrived(ref, sem):
    pltpu.make_async_copy(ref, ref, sem).wait()


def kernel(q, g, o, k, v, xin, dqo, dko, dvo, wo,
           kv, kt, qr, gr, dr, xl, dl, qn, gn, rs, sh, S, E, dka, dva, dqt, partk, partv, rcvk, rcvv, fink, finv,
           xp, xr, xt, dvall, wrc, wrp, w3, wrh, *sems):
    (lg, lo), sk, sv, sq, sg, sd, sx, sb, sc, sc2, sdq, spk, spv, srk, srv, sdv, swc, swp, swh = [
        sems[i:i + 2] for i in range(0, 38, 2)]
    x, z, y, h, c = (lax.axis_index(a) for a in ("x", "z", "y", "h", "c"))
    me = 8 * x + 4 * z + y

    def mod4(i):
        return lax.rem(i + 4, 4)

    xs = [mod4(x + d) for d in range(4)]
    ys = [mod4(y + e) for e in range(4)]
    hs = [mod4(h + e) for e in range(4)]
    near = [(dz, e) for dz in range(2) for e in range(4) if dz or e]

    def in_plane(dz, e):
        return {"z": (1 - z) if dz else z, "y": ys[e]}

    def in_side(dz, d):
        return {"x": xs[d], "z": (1 - z) if dz else z}

    barrier = pltpu.get_barrier_semaphore()
    friends = [{"x": xs[d], "y": ys[e]} for d in range(4) for e in range(4) if d or e]
    friends += [in_plane(1, e) for e in range(4)] + [in_side(1, d) for d in (1, 2, 3)]
    friends += [{"c": 1 - c}] + [{"h": hs[e]} for e in (1, 2, 3)]
    for friend in friends:
        pl.semaphore_signal(barrier, inc=1, device_id=friend, device_id_type=pl.DeviceIdType.MESH)
    get_g = [pltpu.make_async_copy(g.at[0, :, cols(j, LANES)], xp.at[j, :, 0:LANES], lg.at[j]) for j in range(4)]
    get_o = pltpu.make_async_copy(o.at[0], xl.at[:, 0:4 * LANES], lo)
    get_x = pltpu.make_async_copy(xin.at[0], xl, lo)
    for copy in get_g:
        copy.start()
    get_o.start()
    pl.semaphore_wait(barrier, len(friends))

    sends = []

    def send(*a):
        copy = remote(*a)
        copy.start()
        sends.append(copy)

    def spread(src, dst, s, width, which):
        for d in which:
            send(src.at[0, :, cols(xs[d], width)], dst, s, d, {"x": xs[d]})

    def stay(src, dst, s, width):
        pltpu.make_async_copy(src.at[0, :, cols(x, width)], dst, s[1].at[0]).start()

    spread(k, kv.at[me, :, 0:D], sk, D, (1, 3, 2))
    spread(v, kv.at[me, :, D:2 * D], sv, D, (1, 3, 2))
    stay(k, kv.at[me, :, 0:D], sk, D)
    stay(v, kv.at[me, :, D:2 * D], sv, D)
    spread(q, qr.at[x], sq, LANES, (1, 3, 2))
    stay(q, qr.at[x], sq, LANES)
    stay(g, gr.at[x], sg, LANES)

    for copy in get_g:
        copy.wait()
    get_o.wait()
    head = lax.broadcasted_iota(jnp.int32, (HEADS, LANES), 0)
    ones = jnp.where(head == lax.broadcasted_iota(jnp.int32, (HEADS, LANES), 1) // D, 1.0, 0.0).astype(bf)
    for j in range(4):
        at = slice(j * LANES, (j + 1) * LANES)
        prod = xp[j, :, 0:LANES].astype(f32) * xl[:, at].astype(f32)
        high = prod.astype(bf)
        low = (prod - high.astype(f32)).astype(bf)
        dl[j] = dot(ones, high, 1, 1) + dot(ones, low, 1, 1)
    get_x.start()
    for d in (1, 3, 2):
        send(dl.at[xs[d]], dr.at[x], sd, d, {"x": xs[d]})
    pltpu.make_async_copy(dl.at[x], dr.at[x], sd[1].at[0]).start()

    def slot(s, zz, yy):
        return kv.at[8 * s + 4 * zz + yy]

    for s in range(4):
        d = mod4(x - s)
        mine = slot(s, z, y)
        arrived(mine.at[:, 0:D], sk[1].at[d])
        arrived(mine.at[:, D:2 * D], sv[1].at[d])
        send(mine, mine, sb, (s, 0), {"z": 1 - z})
        for e in (1, 3, 2):
            send(mine, mine, sc, (s, e), {"y": ys[e]})

    get_x.wait()
    for j in range(4):
        xp[j] = jnp.concatenate([xl[:, 640 * b + 160 * j:640 * b + 160 * j + 160] for b in range(8)], axis=1)
    dka[...] = jnp.zeros_like(dka)
    dqt[...] = jnp.zeros_like(dqt)

    for s in (0, 1):
        theirs = slot(s + 2, 1 - z, y)
        arrived(theirs, sb[1].at[s + 2, 0])
        for e in (1, 3, 2):
            send(theirs, theirs, sc2, (s + 2, e), {"y": ys[e]})
        for e in (1, 3, 2):
            theirs = slot(s, z, mod4(y - e))
            arrived(theirs, sc[1].at[s, e])
            send(theirs, theirs, sb, (s, e), {"z": 1 - z})
    spread(g, gr.at[x], sg, LANES, (1, 3, 2))
    for e in (1, 3, 2):
        remote(xp.at[ys[e]], xr.at[y], sx, e, {"y": ys[e]}).start()
    pltpu.make_async_copy(xp.at[y], xr.at[y], sx[1].at[0]).start()

    def chunk_of(ch):
        return pl.ds(ch * BLOCKS, BLOCKS)

    def stats(s, carry):
        d = mod4(x - s)
        i = 8 * s + 4 * z + y

        @pl.when(s < 2)
        def _():
            for e in range(4):
                arrived(slot(s, 1 - z, mod4(y - e)), sb[1].at[s, e])

        @pl.when(s >= 2)
        def _():
            for e in (1, 2, 3):
                arrived(slot(s, z, mod4(y - e)), sc[1].at[s, e])
                arrived(slot(s, 1 - z, mod4(y - e)), sc2[1].at[s, e])

        for b in range(8):
            kt[:, cols(8 * s + b, D)] = kv[8 * s + b, :, 0:D].T
        arrived(qr.at[s], sq[1].at[d])
        arrived(dr.at[s], sd[1].at[d])
        for n in range(HEADS):
            cs = slice(n * D, (n + 1) * D)
            qn[s, cs, :] = qr[s, :, cs]
        n = 2 * s + z

        def half(side, carry):
            lanes = cols(side, HALF)

            def rows_of(ch, count, first=0):
                return pl.ds(pl.multiple_of((first + ch) * CHUNK, CHUNK), count * CHUNK)

            def score(ch, count):
                keys = kv[pl.ds(ch * BLOCKS, count * BLOCKS), :, 0:D].reshape(count * CHUNK, D)
                return dot(keys, qn[s, lanes, :], 1, 1)

            def top(m, t):
                return jnp.maximum(m, jnp.max(t.reshape(-1, 8, HALF), axis=0))

            def p1(ch, m, count):
                t = score(ch, count)
                S[rows_of(ch, count), :] = t
                return top(m, t)

            m = lax.fori_loop(0, s, lambda p, m: p1(2 * p, m, 2), jnp.full((8, HALF), -1e30, f32))
            m = lax.fori_loop(2 * s, n, lambda ch, m: p1(ch, m, 1), m)
            last = score(n, 1)
            key = n * CHUNK + lax.broadcasted_iota(jnp.int32, (CHUNK, 1), 0)
            row = i * ROWS + lax.broadcasted_iota(jnp.int32, (1, HALF), 1) % ROWS
            last = jnp.where(key <= row, last, -1e30)
            S[rows_of(n, 1), :] = last
            mc = jnp.max(top(m, last), axis=0, keepdims=True) * LOG

            def p2(ch, total, count):
                e = jnp.exp2(S[rows_of(ch, count), :] * LOG - mc)
                E[rows_of(ch, count, s * (s + 1)), lanes] = e.astype(bf)
                return total + jnp.sum(e.reshape(-1, 8, HALF), axis=0)

            total = lax.fori_loop(0, s, lambda p, t: p2(2 * p, t, 2), jnp.zeros((8, HALF), f32))
            total = lax.fori_loop(2 * s, n + 1, lambda ch, t: p2(ch, t, 1), total)
            rs[s, :, lanes] = 1.0 / jnp.sum(total, axis=0, keepdims=True)
            return carry

        lax.fori_loop(0, 2, half, 0)
        sh[s] = jnp.concatenate([dr[s, a:a + 1, :] for a in range(HEADS)], axis=1) * rs[s]
        return carry

    def scale(s, carry):
        arrived(gr.at[s], sg[1].at[mod4(x - s)])
        heads = jnp.concatenate([rs[s, :, n * D:(n + 1) * D] for n in range(HEADS)], axis=0).T
        for n in range(HEADS):
            cs = slice(n * D, (n + 1) * D)
            gn[s, cs, :] = (gr[s, :, cs].astype(f32) * heads[:, n:n + 1]).astype(bf)
        return carry

    def grads(s, ch, e32):
        at = cols(ch, CHUNK)
        values = kv[chunk_of(ch), :, D:2 * D].reshape(CHUNK, D)
        ds = (e32 * (dot(values, gn[s], 1, 1) - sh[s])).astype(bf)
        dka[at, :] += dot(ds, qn[s], 1, 0)
        dqt[s] += dot(kt[:, at], ds, 1, 0)

    def narrow(s, first, end):
        def one(ch, carry):
            grads(s, ch, E[cols(s * (s + 1) + ch, CHUNK), :].astype(f32))
            return carry

        lax.fori_loop(first, end, one, 0)

    def give_dq(s):
        for n in range(HEADS):
            cs = slice(n * D, (n + 1) * D)
            xl[:, cols(s * HEADS + n, D)] = (dqt[s, :, cs] * SCALE).astype(bf).T
        home = dqo.at[0, :, cols(x, LANES)]

        @pl.when(s == x)
        def _():
            pltpu.make_async_copy(xl.at[:, cols(s, LANES)], home, sdq[1].at[0]).start()

        @pl.when(s != x)
        def _():
            remote(xl.at[:, cols(s, LANES)], home, sdq, mod4(s - x), {"x": s}).start()

    def total_of(part, rcv, sems, s):
        def add(n, total):
            arrived(rcv.at[n, s], sems[1].at[n, s])
            return total + rcv[n, s].astype(f32)

        return lax.fori_loop(1, 8, add, part[s, 4 * z + y].astype(f32)).astype(bf)

    def deliver(src, dst, s2, at, there, s):
        @pl.when(s == x)
        def _():
            pltpu.make_async_copy(src, dst, s2[1].at[there]).start()

        @pl.when(s != x)
        def _():
            remote(src, dst, s2, at, {"x": s}, there).start()

    def reduce_v(s):
        finv[s] = total_of(partv, rcvv, spv, s)
        place = dvall.at[y, :, cols(x, D)]
        for e in (1, 3, 2):
            remote(finv.at[s], place, sdv, (s, e), {"x": s, "y": ys[e]}, (x, y)).start()
        deliver(finv.at[s], place, sdv, (s, 0), (x, y), s)

    def reduce_k(s):
        fink[s] = total_of(partk, rcvk, spk, s)
        deliver(fink.at[s], dko.at[0, :, cols(x, D)], srk, s, x, s)

    def hand_out(part, rcv, sems, a):
        def one(n, carry):
            to = {"z": lax.rem(z + n // 4, 2), "y": lax.rem(y + n, 4)}
            remote(part.at[a, 4 * to["z"] + to["y"]], rcv.at[n, a], sems, (n, a), to).start()
            return carry

        lax.fori_loop(1, 8, one, 0)

    def values_of(t, carry):
        a = 3 - t

        def share(s, ch, count):
            e = E[pl.ds(pl.multiple_of((s * (s + 1) + ch) * CHUNK, CHUNK), count * CHUNK), :]
            return dot(e, gn[s], 1, 0)

        dva[...] = jnp.zeros_like(dva)

        def both(s, carry):
            dva[...] += share(s, 2 * a, 2)
            return carry

        def one(zz, carry):
            dva[cols(zz, CHUNK), :] += share(a, 2 * a + zz, 1)
            return carry

        lax.fori_loop(a + 1, 4, both, 0)
        lax.fori_loop(0, 1 + z, one, 0)
        for b in range(8):
            partv[a, b] = dva[b * ROWS:(b + 1) * ROWS, :].astype(bf)
        hand_out(partv, rcvv, spv, a)
        return carry

    order = [(1, 2), (1, 1), (1, 3), (0, 2), (0, 1), (0, 3), (1, 0), (0, 0)]

    def piece(dz, d):
        peer = in_side(dz, d)
        return peer, 2 * peer["x"] + peer["z"]

    def turn_x():
        line = lax.broadcasted_iota(jnp.int32, (320, 640), 0)
        want = line + 20 * lax.shift_right_logical(line * 3277, 16)
        place = lax.broadcasted_iota(jnp.int32, (320, 640), 1)
        for e in range(4):
            arrived(xr.at[mod4(y - e)], sx[1].at[e])
        def turn(n, carry):
            part_c, half, j = n // 8, n // 4 % 2, n % 4
            pick = jnp.where(place == want + 20 * part_c, 1.0, 0.0).astype(bf)
            rows = dot(pick, xr[j, :, cols(half, 640)], 1, 1).astype(bf)
            xt[part_c, pl.ds(half * 4, 4), :, cols(j, ROWS)] = rows.reshape(4, 80, ROWS)
            return carry

        lax.fori_loop(0, 16, turn, 0)

    def weigh():
        def wait(n, carry):
            arrived(dvall.at[n % 4, :, cols(n // 4, D)], sdv[1].at[n // 4, n % 4])
            return carry

        lax.fori_loop(0, 16, wait, 0)
        tall = dvall[...].reshape(4 * ROWS, 4 * D)

        def product(n, carry):
            half = (1 - c) + n * (2 * c - 1)
            xt[half] = dot(xt[half].reshape(640, 4 * ROWS), tall, 1, 0).astype(bf).reshape(8, 80, 4 * D)

            @pl.when(n == 0)
            def _():
                for m, (dz, d) in enumerate(order):
                    b = piece(dz, d)[1]
                    remote(xt.at[1 - c, b], wrc.at[b], swc, m, {"c": 1 - c}).start()

            return carry

        lax.fori_loop(0, 2, product, 0)

    def over_sides():
        for n, (dz, d) in enumerate(order):
            peer, b = piece(dz, d)
            arrived(wrc.at[b], swc[1].at[n])
            wrc[b] = (xt[c, b].astype(f32) + wrc[b].astype(f32)).astype(bf)
            if dz or d:
                remote(wrc.at[b], wrp.at[dz * 4 + d], swp, dz * 4 + d, peer).start()

    def over_rest():
        total = wrc[2 * x + z].astype(f32)
        for dz, d in near:
            n = dz * 4 + d
            arrived(wrp.at[n], swp[1].at[n])
            total = total + wrp[n].astype(f32)
        for e in range(4):
            w3[e] = jnp.concatenate([total[20 * e:20 * e + 20], jnp.zeros((12, 4 * D), f32)], axis=0).astype(bf)
        for e in (1, 3, 2):
            remote(w3.at[hs[e]], wrh.at[e], swh, e, {"h": hs[e]}).start()

    def give_two(first):
        lax.fori_loop(first, first + 2, lambda s, carry: (give_dq(s), carry)[1], 0)

    def give_early():
        def one(s, carry):
            deliver(finv.at[s], dvo.at[0, :, cols(x, D)], srv, s, x, s)
            return carry

        lax.fori_loop(0, 4, one, 0)
        give_two(0)

    def step(t, carry):
        early = 1 - jnp.minimum(t // 2, 1)
        a = (1 - early) * (3 - (t - 2) // 2)
        s = early * t + (1 - early) * (3 - t % 2)
        narrow(s, 2 * a, jnp.minimum(2 * a + 2 + 2 * early, 2 * s + 1 + z))

        @pl.when(t == 0)
        def _():
            lax.fori_loop(0, 4, lambda n, carry: (reduce_v(3 - n), carry)[1], 0)

        @pl.when(jnp.logical_and(t > 1, t % 2 == 1))
        def _():
            def one(b, carry):
                partk[a, b] = (dka[cols(8 * a + b, ROWS), :] * SCALE).astype(bf)
                return carry

            lax.fori_loop(0, 8, one, 0)
            hand_out(partk, rcvk, spk, a)

        @pl.when(jnp.logical_and(t > 4, t % 2 == 1))
        def _():
            reduce_k(a + 1)


        pl.when(t == 1)(weigh)
        pl.when(t == 3)(over_sides)
        pl.when(t == 3)(give_early)
        pl.when(t == 8)(over_rest)
        return carry

    lax.fori_loop(0, 4, stats, 0)
    lax.fori_loop(0, 4, scale, 0)
    lax.fori_loop(0, 4, values_of, 0)
    turn_x()
    lax.fori_loop(0, 10, step, 0)
    give_two(2)
    reduce_k(0)
    last = w3[h].astype(f32)
    for e in (1, 3, 2):
        arrived(wrh.at[e], swh[1].at[e])
        last = last + wrh[e].astype(f32)
    wo[...] = last[0:20]

    for d in range(4):
        f = mod4(x - d)
        arrived(dqo.at[0, :, cols(f, LANES)], sdq[1].at[d])
        arrived(dko.at[0, :, cols(d, D)], srk[1].at[d])
        arrived(dvo.at[0, :, cols(d, D)], srv[1].at[d])
    for copy in sends:
        copy.wait_send()
    for e in (1, 2, 3):
        remote(xp.at[ys[e]], xr.at[y], sx, e, {"y": ys[e]}).wait_send()
    for d in (1, 2, 3):
        remote(xl.at[:, cols(xs[d], LANES)], dqo.at[0, :, cols(x, LANES)], sdq, d, {"x": xs[d]}).wait_send()
    def sent(n, carry):
        to = {"z": lax.rem(z + n // 4, 2), "y": lax.rem(y + n, 4)}
        for a in range(4):
            remote(partk.at[a, 0], rcvk.at[n, a], spk, (n, a), to).wait_send()
            remote(partv.at[a, 0], rcvv.at[n, a], spv, (n, a), to).wait_send()
        return carry

    lax.fori_loop(1, 8, sent, 0)
    for s in range(4):
        for e in (1, 2, 3):
            remote(finv.at[s], dvall.at[y, :, cols(x, D)], sdv, (s, e), {"y": ys[e]}).wait_send()
    for d in (1, 2, 3):
        t = xs[d]
        remote(finv.at[t], dvall.at[y, :, cols(x, D)], sdv, (t, 0), {"x": t}).wait_send()
        remote(fink.at[t], dko.at[0, :, cols(x, D)], srk, t, {"x": t}).wait_send()
        remote(finv.at[t], dvo.at[0, :, cols(x, D)], srv, t, {"x": t}).wait_send()
    for n, (dz, d) in enumerate(order):
        peer, b = piece(dz, d)
        remote(xt.at[1 - c, b], wrc.at[b], swc, n, {"c": 1 - c}).wait_send()
        if dz or d:
            remote(wrc.at[b], wrp.at[dz * 4 + d], swp, dz * 4 + d, peer).wait_send()
    for e in (1, 2, 3):
        remote(w3.at[hs[e]], wrh.at[e], swh, e, {"h": hs[e]}).wait_send()


def per_device(x_in, q, k, v, o, g):
    T = 32 * ROWS
    anyspace = pl.BlockSpec(memory_space=pl.ANY)
    sems = [(4,), ()] + [(4,)] * 12 + [(4, 4)] * 6 + [(4,)] * 2 + [(8, 4)] * 4 + [(4,)] * 4 + [(4, 4)] * 2 + [(8,)] * 2
    sems += [(8,)] * 2 + [(4,)] * 2
    tall = (T, D)
    scratch = [((32, ROWS, 2 * D), bf), ((D, T), bf), ((4, ROWS, LANES), bf), ((4, ROWS, LANES), bf), ((4, HEADS, ROWS), f32),
               ((ROWS, 4 * XCOLS), bf), ((4, HEADS, ROWS), f32),
               ((4, LANES, D), bf), ((4, LANES, D), bf), ((4, 1, LANES), f32), ((4, 1, LANES), f32),
               ((T, HALF), f32), ((20 * CHUNK, LANES), bf), (tall, f32), ((2 * CHUNK, D), f32), ((4, D, LANES), f32),
               ((4, 8, ROWS, D), bf), ((4, 8, ROWS, D), bf), ((8, 4, ROWS, D), bf),
               ((8, 4, ROWS, D), bf), ((4, ROWS, D), bf), ((4, ROWS, D), bf),
               ((4, ROWS, XCOLS), bf), ((4, ROWS, XCOLS), bf), ((2, 8, 80, 4 * ROWS), bf), ((4, ROWS, 4 * D), bf),
               ((8, 80, 4 * D), bf), ((8, 80, 4 * D), bf),
               ((4, 32, 4 * D), bf), ((4, 32, 4 * D), bf)]
    return pl.pallas_call(
        kernel,
        out_shape=[jax.ShapeDtypeStruct((1, ROWS, 4 * LANES), bf), jax.ShapeDtypeStruct((1, ROWS, 4 * D), bf),
                   jax.ShapeDtypeStruct((1, ROWS, 4 * D), bf), jax.ShapeDtypeStruct((20, 4 * D), f32)],
        in_specs=[anyspace] * 6,
        out_specs=[anyspace] * 3 + [pl.BlockSpec(memory_space=pltpu.VMEM)],
        scratch_shapes=[pltpu.VMEM(*s) for s in scratch] + [pltpu.SemaphoreType.DMA(s) for s in sems],
        compiler_params=pltpu.CompilerParams(vmem_limit_bytes=60 << 20, collective_id=0, has_side_effects=True),
        name="attention_backward")(q, g, o, k, v, x_in)


def solution(mesh):
    fine = Mesh(mesh.devices.reshape(4, 2, 4, 4, 2), ("x", "z", "y", "h", "c"))
    seq, dp = ("x", "z", "y"), ("h", "c")
    rows = P(dp, seq, None)
    return jax.shard_map(per_device, mesh=fine, in_specs=(rows,) * 6,
                         out_specs=(rows, rows, rows, P(seq + dp, None)), check_vma=False)
```
